128 devices in a mesh: ctx: 4 (over z_lo, core), resp: 32 (over z_hi, y, x).
Axes of the slice: x: 4, y: 4, z: 4 (z_hi: 2, z_lo: 2; z = z_hi * 2 + z_lo), core: 2. Of those that a mesh axis runs over, the one named last changes fastest.
Arguments:
- prompt_q: bfloat16 [32, 768, 4096], P('resp', 'ctx'), may hold values from -6 to 6
- prompt_kv: bfloat16 [32, 768, 1024], P('resp', 'ctx'), may hold values from -6 to 6
- prompt_cot: bfloat16 [32, 768, 4096], P('resp', 'ctx'), may hold values from -6 to 6
- resp_q: bfloat16 [128, 64, 4096], P('resp'), may hold values from -6 to 6
- resp_kv: bfloat16 [128, 64, 1024], P('resp'), may hold values from -6 to 6
- resp_cot: bfloat16 [128, 64, 4096], P('resp'), may hold values from -6 to 6
- resp_prompt: int32 [128, 1], P('resp'), may hold values from 0 to 31
- tree_end: int32 [128, 64], P('resp'), may hold values from 2 to 64, as said below
- rewards: int32 [128], P('resp'), may hold values from 0 to 10
Outputs:
- d_prompt_q: bfloat16 [32, 768, 4096], P('resp', 'ctx')
- d_prompt_kv: bfloat16 [32, 768, 1024], P('resp', 'ctx')
- d_resp_q: bfloat16 [128, 64, 4096], P('resp')
- d_resp_kv: bfloat16 [128, 64, 1024], P('resp')
The draws below stay inside these ranges and needn't reach their ends.
Inputs may be any that keep to these rules, and one draw needn't show every extreme that they name: `resp_prompt`: every prompt is the prompt of at least one response. Each response tree's tokens stand in depth-first order with token 0 as its only root: tree_end[i, u] > u, token 0's entry is 64, and the spans of two tokens are nested or apart.
All inputs are finite; a program needn't handle non-finite values.
Results may differ from the reference program's by a relative error of at most 0.029.
Values may be sent and summed in bfloat16 or wider, within the bound.
A program may use at most 192 MiB of HBM per device.

```python
import math
import jax
import jax.numpy as jnp
from jax import lax

HEADS = 32
KV_HEADS = 4
HEAD_DIM = 128
R_DEV = 4
RLEN = 64
PLEN = 768
PROMPTS = 32
RESPONSES = 128


def drawn_entries(key, shape):
    return jnp.clip(jax.random.normal(key, shape, jnp.float32), -6.0, 6.0)


def rising_keys(values, start, finish):
    places = jnp.arange(PLEN, dtype=jnp.float32)
    ramp = start + (finish - start) * places / (PLEN - 1)
    shaped = values.reshape(PROMPTS, PLEN, 2, KV_HEADS * HEAD_DIM)
    halves = jnp.where(jnp.arange(2, dtype=jnp.int32) == 0, 1.0, 0.0).astype(jnp.float32)
    factor = 1.0 + halves[None, None, :, None] * (ramp[None, :, None, None] - 1.0)
    return jnp.clip(shaped * factor, -6.0, 6.0).reshape(values.shape)


def draw_prompt_q(key, part):
    key = jax.random.fold_in(key, 21)
    shape = (PROMPTS, PLEN, HEADS * HEAD_DIM)
    values = drawn_entries(key, shape)
    return values.astype(jnp.bfloat16)


def draw_resp_q(key, part):
    key = jax.random.fold_in(key, 23)
    shape = (RESPONSES, RLEN, HEADS * HEAD_DIM)
    values = drawn_entries(key, shape)
    return values.astype(jnp.bfloat16)


def draw_prompt_kv(key, part):
    key = jax.random.fold_in(key, 22)
    shape = (PROMPTS, PLEN, 2 * KV_HEADS * HEAD_DIM)
    values = rising_keys(drawn_entries(key, shape), 0.5, 2.0)
    return values.astype(jnp.bfloat16)


def draw_tree_end(key, part):
    key = jax.random.fold_in(key, 11)
    climbs = jax.random.randint(key, (RLEN, RESPONSES), 0, 10)
    returns = jax.random.randint(jax.random.fold_in(key, 1), (RLEN, RESPONSES), 0, 1 << 20)

    def advance(level, pieces):
        climbed, chosen = pieces
        lowered = 1 + chosen % jnp.maximum(level, 1)
        updated = jnp.where(climbed < 8, level + 1, lowered)
        return (updated, updated)
    start_level = jnp.zeros((RESPONSES,), jnp.int32)
    unused, levels = lax.scan(advance, start_level, (climbs[1:], returns[1:]))
    levels = jnp.concatenate([start_level[None, :], levels], axis=0).T
    places = jnp.arange(RLEN, dtype=jnp.int32)
    beyond = (places[None, None, :] > places[None, :, None]) & (levels[:, None, :] <= levels[:, :, None])
    return jnp.min(jnp.where(beyond, places[None, None, :], RLEN), axis=2).astype(jnp.int32)


def touch_ends(drawn, stream_key, smallest, largest):
    longest = drawn.shape.index(max(drawn.shape))
    spots = []
    for shift in (0, 1):
        where = [jax.random.randint(jax.random.fold_in(stream_key, axis), (), 0, length) for axis, length in enumerate(drawn.shape)]
        where[longest] = (where[longest] + shift) % drawn.shape[longest]
        spots.append(tuple(where))
    return drawn.at[spots[0]].set(smallest).at[spots[1]].set(largest)


def shard_levels(key, shape, cuts, smallest, high):
    level = 1.0
    for dim, blocks in cuts:
        draws = jax.random.uniform(jax.random.fold_in(jax.random.fold_in(key, 6), dim), (blocks,), jnp.float32, smallest / len(cuts), high / len(cuts))
        level = level * jnp.repeat(jnp.exp(draws), shape[dim] // blocks).reshape((-1,) + (1,) * (len(shape) - 1 - dim))
    return level


def distinct(own_key, rows, number_of, top, lift):
    order = jax.random.permutation(jax.random.fold_in(own_key, 1), number_of)
    pull = order
    for power in range(3):
        pull = pull * pull // number_of
    pull = pull * lift // number_of
    chance = jax.random.randint(jax.random.fold_in(own_key, 2), (rows, number_of), 0, 4096) + pull
    sure = jax.random.permutation(jax.random.fold_in(own_key, 3), rows)[jnp.arange(number_of) % rows]
    chance = jnp.where(jnp.arange(rows)[:, None] == sure[None, :], 1 << 14, chance)
    priority = chance * number_of + jnp.arange(number_of)
    return lax.top_k(priority.astype(jnp.int32), top)[1].astype(jnp.int32)


def scatter_about(rng, dims, scale, limit, split=(), kind=jnp.bfloat16):
    array = jax.random.normal(rng, dims, jnp.float32) * scale
    if len(split) > 0:
        array = shard_levels(rng, dims, split, -0.22, 0.18) * array
    return jnp.clip(array, min=-limit, max=limit).astype(kind)


def setup_inputs(seed: int = 0) -> dict:
    streams_of = jax.random.split(jax.random.key(seed), 10)
    return {
        "prompt_q": draw_prompt_q(jax.random.fold_in(streams_of[9], 71), 0),
        "prompt_kv": draw_prompt_kv(jax.random.fold_in(streams_of[9], 71), 0),
        "prompt_cot": scatter_about(streams_of[2], (PROMPTS, PLEN, HEADS * HEAD_DIM), 1.0, 6.0, ((0, 32), (1, 4))),
        "resp_q": draw_resp_q(jax.random.fold_in(streams_of[9], 71), 0),
        "resp_kv": scatter_about(streams_of[4], (RESPONSES, RLEN, 2 * KV_HEADS * HEAD_DIM), 1.0, 6.0, ((0, 32),)),
        "resp_cot": scatter_about(streams_of[5], (RESPONSES, RLEN, HEADS * HEAD_DIM), 1.0, 6.0, ((0, 32),)),
        "resp_prompt": distinct(streams_of[6], RESPONSES, PROMPTS, 1, 512),
        "tree_end": draw_tree_end(jax.random.fold_in(streams_of[9], 71), 0),
        "rewards": touch_ends(jax.random.randint(streams_of[8], (RESPONSES,), 0, 11), jax.random.fold_in(streams_of[8], 1), 0, 10).astype(jnp.int32),
    }


def rounded(values):
    return lax.optimization_barrier(values.astype(jnp.bfloat16)).astype(jnp.float32)

def attend_grads(queries, key_value, allowed, cotangent):
    scaling = 1.0 / math.sqrt(HEAD_DIM)
    kv_width = KV_HEADS * HEAD_DIM
    row_count = queries.shape[0]
    key_count = key_value.shape[0]
    query_heads = queries.astype(jnp.float32).reshape(row_count, KV_HEADS, HEADS // KV_HEADS, HEAD_DIM)
    key_heads = key_value[:, :kv_width].astype(jnp.float32).reshape(key_count, KV_HEADS, HEAD_DIM)
    value_heads = key_value[:, kv_width:].astype(jnp.float32).reshape(key_count, KV_HEADS, HEAD_DIM)
    grad_heads = cotangent.astype(jnp.float32).reshape(query_heads.shape)
    scores = jnp.einsum('nkgd,mkd->kgnm', query_heads, key_heads) * scaling
    scores = jnp.where(allowed[None, None], scores, -jnp.inf)
    highest = lax.optimization_barrier(jnp.max(scores, axis=-1, keepdims=True))
    totals = lax.optimization_barrier(jnp.sum(jnp.exp(scores - highest), axis=-1, keepdims=True))
    log_total = highest + jnp.log(totals)
    weights = jnp.exp(scores - log_total)
    narrow_weights = rounded(weights)
    output = jnp.einsum('kgnm,mkd->nkgd', narrow_weights, value_heads)
    row_delta = jnp.transpose(lax.optimization_barrier(jnp.sum(grad_heads * output, axis=-1)), (1, 2, 0))
    grad_prob = jnp.einsum('nkgd,mkd->kgnm', grad_heads, value_heads)
    grad_score = rounded(weights * (grad_prob - row_delta[..., None]))
    grad_query = jnp.einsum('kgnm,mkd->nkgd', grad_score, key_heads) * scaling
    grad_keys = jnp.einsum('kgnm,nkgd->mkd', grad_score, query_heads) * scaling
    grad_values = jnp.einsum('kgnm,nkgd->mkd', narrow_weights, grad_heads)
    grad_rows = jnp.concatenate([grad_keys.reshape(key_count, kv_width), grad_values.reshape(key_count, kv_width)], axis=1)
    return (grad_query.reshape(row_count, HEADS * HEAD_DIM), grad_rows)

def reference(prompt_q, prompt_kv, prompt_cot, resp_q, resp_kv, resp_cot, resp_prompt, tree_end, rewards):
    routes = resp_prompt[:, 0].astype(jnp.int32)
    onehot = (routes[:, None] == jnp.arange(PROMPTS, dtype=jnp.int32)[None, :]).astype(jnp.float32)
    reward_values = rewards.astype(jnp.float32)
    counts = lax.optimization_barrier(jnp.sum(onehot, axis=0))
    reward_sums = lax.optimization_barrier(jnp.sum(onehot * reward_values[:, None], axis=0))
    reward_squares = lax.optimization_barrier(jnp.sum(onehot * (reward_values * reward_values)[:, None], axis=0))
    means = reward_sums / counts
    spread = jnp.sqrt(reward_squares * counts - reward_sums * reward_sums) / counts
    advantage = (reward_values - lax.optimization_barrier(jnp.sum(onehot * means[None, :], axis=1))) / jnp.maximum(lax.optimization_barrier(jnp.sum(onehot * spread[None, :], axis=1)), 1.0)
    positions = jnp.arange(PLEN, dtype=jnp.int32)
    causal = positions[None, :] <= positions[:, None]

    def prompt_one(bundle):
        return attend_grads(bundle[0], bundle[1], causal, bundle[2])
    self_grad_q, self_grad_kv = lax.map(prompt_one, (prompt_q, prompt_kv, prompt_cot))

    def response_one(bundle):
        queries, own_rows, cotangent, prompt_index, tree_ends, weight = bundle
        key_value = jnp.concatenate([prompt_kv[prompt_index], own_rows], axis=0)
        places = jnp.arange(RLEN, dtype=jnp.int32)
        tree_mask = (places[None, :] <= places[:, None]) & (places[:, None] < tree_ends[None, :])
        allowed = jnp.concatenate([jnp.ones((RLEN, PLEN), dtype=jnp.bool_), tree_mask], axis=1)
        scaled = (weight * cotangent.astype(jnp.float32)).astype(jnp.bfloat16)
        grad_query, grad_rows = attend_grads(queries, key_value, allowed, scaled)
        return (grad_query, grad_rows[:PLEN], grad_rows[PLEN:])

    def to_blocks(values):
        return values.reshape((PROMPTS, R_DEV) + values.shape[1:])

    def block_step(running, bundle):
        grad_query, prompt_terms, tree_terms = lax.map(response_one, bundle[:6])
        shares = jnp.einsum('rp,rmx->pmx', bundle[6], prompt_terms, precision=lax.Precision.HIGHEST)
        return (running + rounded(shares), (grad_query, tree_terms))
    inputs = tuple((to_blocks(values) for values in (resp_q, resp_kv, resp_cot, routes, tree_end, advantage, onehot)))
    initial = jnp.zeros((PROMPTS, PLEN, 2 * KV_HEADS * HEAD_DIM), jnp.float32)
    running, (grad_resp_q, tree_grad) = lax.scan(block_step, initial, inputs)
    d_prompt_q = self_grad_q.astype(jnp.bfloat16)
    d_prompt_kv = (self_grad_kv + running).astype(jnp.bfloat16)
    d_resp_q = grad_resp_q.reshape(RESPONSES, RLEN, HEADS * HEAD_DIM).astype(jnp.bfloat16)
    d_resp_kv = tree_grad.reshape(RESPONSES, RLEN, 2 * KV_HEADS * HEAD_DIM).astype(jnp.bfloat16)
    return (d_prompt_q, d_prompt_kv, d_resp_q, d_resp_kv)
```

```python
import functools
import math

import jax
import jax.numpy as jnp
from jax import lax
from jax.experimental import pallas as pl
from jax.experimental.pallas import tpu as pltpu
from jax.sharding import PartitionSpec as P

MESH = pl.DeviceIdType.MESH
KV_HEADS = 4
HEAD_DIM = 128
CTX = 4
ROUTE_ROW = 4
REWARD_ROW = 5


def dot_nt(a, b):
    return lax.dot_general(a, b, (((1,), (1,)), ((), ())), preferred_element_type=jnp.float32)


def dot_tn(a, b):
    return lax.dot_general(a, b, (((0,), (0,)), ((), ())), preferred_element_type=jnp.float32)


def dot_nn(a, b):
    return lax.dot_general(a, b, (((1,), (0,)), ((), ())), preferred_element_type=jnp.float32)


def aligned(start, size):
    return pl.ds(pl.multiple_of(start, 16), size)


def columns(start, size):
    return pl.ds(pl.multiple_of(start, 128), size)


def attention_grads(queries, cotangent, pieces, scale):
    to_power = scale * math.log2(math.e)
    scores = []
    for keys, values, adjust in pieces:
        part = dot_nt(keys, queries) * to_power
        scores.append(part if adjust is None else adjust(part))
    highest = functools.reduce(
        jnp.maximum, [jnp.max(part, axis=0, keepdims=True) for part in scores]
    )
    powers = [jnp.exp2(part - highest) for part in scores]
    total = functools.reduce(jnp.add, [jnp.sum(part, axis=0, keepdims=True) for part in powers])
    inverse = 1.0 / total
    grad_probs = [dot_nt(values, cotangent) for keys, values, adjust in pieces]
    delta = inverse * functools.reduce(
        jnp.add,
        [jnp.sum(a * b, axis=0, keepdims=True) for a, b in zip(powers, grad_probs)],
    )
    grad_query = None
    grads = []
    for (keys, values, adjust), power, grad_prob in zip(pieces, powers, grad_probs):
        weight = power * inverse
        narrow = weight.astype(jnp.bfloat16)
        grad_score = (weight * (grad_prob - delta)).astype(jnp.bfloat16)
        grad_values = dot_nn(narrow, cotangent)
        grad_keys = dot_nn(grad_score, queries)
        term = dot_tn(keys, grad_score)
        grad_query = term if grad_query is None else grad_query + term
        grads.append((grad_keys, grad_values))
    return grad_query, grads


def kernel(
    ring,
    routes_in,
    rewards_in,
    tree_in,
    pq,
    pkv,
    pcot,
    rq,
    rkv,
    rcot,
    dpq,
    dpkv,
    drq,
    drkv,
    pq_v,
    pcot_v,
    tiles,
    rq_v,
    rcot_v,
    tree_k,
    tree_v,
    notes,
    picks_v,
    picks,
    pieces_in,
    picked,
    chosen,
    bias,
    self_acc,
    self_out,
    self_in,
    dpq_v,
    grads,
    shares,
    share_acc,
    totals,
    returned,
    drq_v,
    dtree_k,
    dtree_v,
    sem_load,
    sem_note,
    sem_piece,
    sem_tile_send,
    sem_tile_recv,
    sem_pick_send,
    sem_pick_recv,
    sem_self_send,
    sem_self_recv,
    sem_share_send,
    sem_share_recv,
    sem_query,
    sem_tree,
    sem_total,
):
    scale = 1.0 / math.sqrt(HEAD_DIM)
    c = lax.axis_index("ctx")
    me = lax.axis_index("resp")
    rows = pq.shape[0]
    length = CTX * rows
    count, tokens = rq.shape[0], rq.shape[1]
    group = pq.shape[1] // (KV_HEADS * HEAD_DIM)
    width = group * HEAD_DIM
    half = KV_HEADS * HEAD_DIM
    size = 2 * length // ring
    blocks = rows // size
    source = lax.rem(me, ring // 2) // blocks
    own_block = lax.rem(me, blocks)
    own_kind = me // (ring // 2)
    beside = c + 1 - 2 * lax.rem(c, 2)
    across = lax.rem(c + 2, CTX)
    x_size = min(4, ring)
    y_size = min(4, ring // x_size)
    z_size = ring // (x_size * y_size)

    def moved(step):
        x = lax.rem(lax.rem(me, x_size) + lax.rem(step, x_size), x_size)
        y = lax.rem(lax.rem(me // x_size, y_size) + lax.rem(step // x_size, y_size), y_size)
        z = lax.rem(me // (x_size * y_size) + step // (x_size * y_size), z_size)
        return (z * y_size + y) * x_size + x

    def remote(src, dst, send, recv, where):
        return pltpu.make_async_remote_copy(
            src_ref=src,
            dst_ref=dst,
            send_sem=send,
            recv_sem=recv,
            device_id=where,
            device_id_type=MESH,
        )

    def settle(ref, sem):
        pltpu.make_async_copy(ref, ref, sem).wait()

    own_columns = columns(c * width, width)
    loads = [
        pltpu.make_async_copy(pq, pq_v, sem_load.at[0]),
        pltpu.make_async_copy(pcot, pcot_v, sem_load.at[1]),
        pltpu.make_async_copy(pkv, tiles.at[aligned(c * rows, rows)], sem_load.at[2]),
        pltpu.make_async_copy(rq.at[:, :, own_columns], rq_v, sem_load.at[3]),
        pltpu.make_async_copy(rcot.at[:, :, own_columns], rcot_v, sem_load.at[4]),
        pltpu.make_async_copy(
            rkv.at[:, :, columns(c * HEAD_DIM, HEAD_DIM)], tree_k, sem_load.at[5]
        ),
        pltpu.make_async_copy(
            rkv.at[:, :, columns(half + c * HEAD_DIM, HEAD_DIM)], tree_v, sem_load.at[6]
        ),
    ]
    for load in loads:
        load.start()

    barrier = pltpu.get_barrier_semaphore()

    def greet(step, carry):
        there = (lax.rem(c + step // ring, CTX), lax.rem(me + lax.rem(step, ring), ring))
        pl.semaphore_signal(barrier, inc=1, device_id=there, device_id_type=MESH)
        return carry

    lax.fori_loop(1, CTX * ring, greet, 0)

    row = lax.broadcasted_iota(jnp.int32, (8, 128), 0)
    lane = lax.broadcasted_iota(jnp.int32, (8, 128), 1)
    note = jnp.zeros((8, 128), jnp.int32)
    inside = lane // 16 == lax.rem(me, 8)
    for r in range(count):
        route = routes_in[r, 0]
        note = jnp.where((row == r) & inside, route * 16 + lane % 16, note)
        note = jnp.where((row == ROUTE_ROW) & (lane == r), route, note)
        note = jnp.where((row == REWARD_ROW) & (lane == r), rewards_in[r], note)
    notes[me] = note

    pl.semaphore_wait(barrier, CTX * ring - 1)

    def send_note(step, carry):
        there = moved(step)
        remote(notes.at[me], notes.at[me], sem_note.at[0], sem_note.at[1], (c, there)).start()
        return carry

    lax.fori_loop(1, ring, send_note, 0)

    def send_piece(step, carry):
        head = lax.rem(c + step, KV_HEADS)
        part = lax.rem(step // KV_HEADS + me, 2 * blocks)
        kind = part // blocks
        block = lax.rem(part, blocks)
        there = kind * (ring // 2) + c * blocks + block
        piece = pkv.at[
            aligned(block * size, size), columns(kind * half + head * HEAD_DIM, HEAD_DIM)
        ]
        here = (head == c) & (there == me)

        @pl.when(here)
        def _():
            pltpu.make_async_copy(piece, pieces_in.at[me], sem_piece.at[2]).start()

        @pl.when(jnp.logical_not(here))
        def _():
            remote(
                piece, pieces_in.at[me], sem_piece.at[0], sem_piece.at[1], (head, there)
            ).start()

        return carry

    lax.fori_loop(0, KV_HEADS * 2 * blocks, send_piece, 0)

    def tile(index):
        return tiles.at[pl.ds(index * rows, rows)]

    def send_tile(src, index, slot, where):
        return remote(src, tile(index), sem_tile_send.at[slot], sem_tile_recv.at[index], (where, me))

    @pl.when(c == 0)
    def _():
        send_tile(pkv, 0, 0, 2).start()
        send_tile(pkv, 0, 1, 1).start()

    @pl.when(c == 1)
    def _():
        send_tile(pkv, 1, 0, 3).start()

    @pl.when(c == 2)
    def _():
        send_tile(pkv, 2, 0, 3).start()

    for index in range(1, CTX):

        @pl.when(c < index)
        def _():
            tiles[index * rows : (index + 1) * rows, :] = jnp.zeros((rows, 2 * half), jnp.bfloat16)

    position = lax.broadcasted_iota(jnp.int32, (length, 2 * rows), 0)
    query = lax.broadcasted_iota(jnp.int32, (length, 2 * rows), 1)
    query = jnp.where(query >= rows, query - rows, query) + c * rows
    bias[...] = jnp.where(position <= query, 0.0, -jnp.inf)
    self_acc[...] = jnp.zeros_like(self_acc)

    settle(notes.at[pl.ds(0, ring - 1)], sem_note.at[1])
    every = notes[...]
    note_row = lax.broadcasted_iota(jnp.int32, every.shape, 1)
    routes = jnp.sum(jnp.where(note_row == ROUTE_ROW, every, 0), axis=1)
    rewards = jnp.sum(jnp.where(note_row == REWARD_ROW, every, 0), axis=1).astype(jnp.float32)
    picks_v[...] = routes
    to_scalars = pltpu.make_async_copy(picks_v, picks, sem_note.at[2])
    to_scalars.start()
    to_scalars.wait()

    @pl.when(c == source)
    def _():
        settle(pieces_in.at[me], sem_piece.at[2])
        settle(pieces_in.at[pl.ds(0, ring - 1)], sem_piece.at[1])

    @pl.when(c != source)
    def _():
        settle(pieces_in, sem_piece.at[1])

    for r in range(count):
        chosen[r, aligned(me * size, size), :] = pieces_in[picks[me, r]]

    def send_pick(step, carry):
        r = step // (ring - 1)
        there = moved(lax.rem(step, ring - 1) + 1)
        picked[r, there] = pieces_in[picks[there, r]]
        remote(
            picked.at[r, there],
            chosen.at[r, aligned(me * size, size)],
            sem_pick_send.at[r],
            sem_pick_recv.at[r],
            (c, there),
        ).start()
        return carry

    lax.fori_loop(0, count * (ring - 1), send_pick, 0)

    @pl.when(c == 2)
    def _():
        settle(tile(0), sem_tile_recv.at[0])
        send_tile(tile(0), 0, 1, 3).start()
        settle(tile(1), sem_tile_recv.at[1])

    @pl.when(c == 3)
    def _():
        settle(tile(1), sem_tile_recv.at[1])
        send_tile(tile(1), 1, 0, 2).start()
        settle(tile(0), sem_tile_recv.at[0])
        settle(tile(2), sem_tile_recv.at[2])

    @pl.when(c == 1)
    def _():
        settle(tile(0), sem_tile_recv.at[0])

    for load in loads:
        load.wait()

    note_lane = lax.broadcasted_iota(jnp.int32, routes.shape, 1)
    for r in range(count):
        same = ((routes == routes_in[r, 0]) & (note_lane < count)).astype(jnp.float32)

        def summed(values):
            return jnp.sum(jnp.sum(values, axis=1, keepdims=True), axis=0, keepdims=True)

        number = summed(same)
        reward_sum = summed(same * rewards)
        reward_square = summed(same * rewards * rewards)
        variance = reward_square * number - reward_sum * reward_sum
        spread = jnp.sqrt(jnp.maximum(variance, number * number)) / number
        own_reward = jnp.full((1, 1), rewards_in[r], jnp.int32).astype(jnp.float32)
        advantage = (own_reward - reward_sum / number) / spread
        rcot_v[r] = (advantage * rcot_v[r].astype(jnp.float32)).astype(jnp.bfloat16)

    def prompt_step(step, carry):
        head = step // (group // 2)
        first = columns(step * 2 * HEAD_DIM, HEAD_DIM)
        second = columns(step * 2 * HEAD_DIM + HEAD_DIM, HEAD_DIM)
        key_columns = columns(head * HEAD_DIM, HEAD_DIM)
        value_columns = columns(half + head * HEAD_DIM, HEAD_DIM)
        queries = jnp.concatenate([pq_v[:, first], pq_v[:, second]], axis=0)
        cotangent = jnp.concatenate([pcot_v[:, first], pcot_v[:, second]], axis=0)
        grad_query, ((grad_keys, grad_values),) = attention_grads(
            queries,
            cotangent,
            [(tiles[:, key_columns], tiles[:, value_columns], lambda part: part + bias[...])],
            scale,
        )
        self_acc[:, key_columns] += grad_keys
        self_acc[:, value_columns] += grad_values
        turned = jnp.transpose(grad_query * scale).astype(jnp.bfloat16)
        dpq_v[:, first] = turned[:rows]
        dpq_v[:, second] = turned[rows:]
        return carry

    lax.fori_loop(0, KV_HEADS * group // 2, prompt_step, 0)
    store_dpq = pltpu.make_async_copy(dpq_v, dpq, sem_load.at[7])
    store_dpq.start()
    self_acc[:, :half] = self_acc[:, :half] * scale

    def self_tile(index):
        return self_acc[index * rows : (index + 1) * rows, :]

    def send_self(values, slot, there, there_slot):
        self_out[slot] = values.astype(jnp.bfloat16)
        remote(
            self_out.at[slot],
            self_in.at[there_slot],
            sem_self_send.at[slot],
            sem_self_recv.at[there_slot],
            (there, me),
        ).start()

    @pl.when(c == 1)
    def _():
        send_self(self_tile(0), 0, 0, 0)

    @pl.when(c == 2)
    def _():
        send_self(self_tile(1), 0, 3, 0)

    @pl.when(c == 3)
    def _():
        send_self(self_tile(0), 0, 2, 0)
        send_self(self_tile(2), 1, 2, 1)

    key_place = lax.broadcasted_iota(jnp.int32, (tokens, group * tokens), 0)
    query_place = lax.broadcasted_iota(jnp.int32, (tokens, group * tokens), 1) % tokens
    square_row = lax.broadcasted_iota(jnp.int32, (tokens, tokens), 0)
    square_column = lax.broadcasted_iota(jnp.int32, (tokens, tokens), 1)

    def stacked(values):
        return jnp.concatenate(
            [values[:, g * HEAD_DIM : (g + 1) * HEAD_DIM] for g in range(group)], axis=0
        )

    def query_rows(r, owner):
        return drq.at[r, :, columns(owner * width, width)]

    def response_step(r, carry):
        settle(chosen.at[r, pl.ds(0, (ring - 1) * size)], sem_pick_recv.at[r])
        ends = tree_in[pl.ds(r, 1), :]
        ends = jnp.sum(
            jnp.where(square_row == square_column, ends, 0), axis=1, keepdims=True
        )
        allowed = (key_place <= query_place) & (query_place < ends)
        queries = stacked(rq_v[r])
        cotangent = stacked(rcot_v[r])
        grad_query, (prompt_terms, tree_terms) = attention_grads(
            queries,
            cotangent,
            [
                (chosen[r, :length, :], chosen[r, length:, :], None),
                (tree_k[r], tree_v[r], lambda part: jnp.where(allowed, part, -jnp.inf)),
            ],
            scale,
        )
        grads[r, :length, :] = (prompt_terms[0] * scale).astype(jnp.bfloat16)
        grads[r, length:, :] = prompt_terms[1].astype(jnp.bfloat16)
        dtree_k[r] = (tree_terms[0] * scale).astype(jnp.bfloat16)
        dtree_v[r] = tree_terms[1].astype(jnp.bfloat16)
        turned = jnp.transpose(grad_query * scale).astype(jnp.bfloat16)
        drq_v[r] = jnp.concatenate(
            [turned[g * tokens : (g + 1) * tokens] for g in range(group)], axis=1
        )

        def send_share(step, inner):
            there = moved(step)
            remote(
                grads.at[r, aligned(there * size, size)],
                shares.at[r, me],
                sem_share_send.at[r],
                sem_share_recv.at[r],
                (c, there),
            ).start()
            return inner

        mine = query_rows(r, c)
        remote(drq_v.at[r], mine, sem_query.at[0, r], sem_query.at[1, r], (across, me)).start()
        lax.fori_loop(1, ring, send_share, 0)
        shares[r, me] = grads[r, aligned(me * size, size), :]
        remote(drq_v.at[r], mine, sem_query.at[2, r], sem_query.at[3, r], (beside, me)).start()
        pltpu.make_async_copy(drq_v.at[r], mine, sem_query.at[6, r]).start()
        return carry

    lax.fori_loop(0, count, response_step, 0)

    def tree_part(kind, owner):
        return drkv.at[:, :, columns(kind * half + owner * HEAD_DIM, HEAD_DIM)]

    tree_copies = []
    for kind, values in ((0, dtree_k), (1, dtree_v)):
        mine = tree_part(kind, c)
        tree_copies.append(
            (
                remote(values, mine, sem_tree.at[0, kind], sem_tree.at[1, kind], (across, me)),
                remote(values, mine, sem_tree.at[2, kind], sem_tree.at[3, kind], (beside, me)),
                pltpu.make_async_copy(values, mine, sem_tree.at[6, kind]),
            )
        )
        for copy in tree_copies[-1]:
            copy.start()

    @pl.when(c == 2)
    def _():
        settle(self_in.at[0], sem_self_recv.at[0])
        send_self(self_tile(0) + self_in[0].astype(jnp.float32), 2, 0, 2)

    @pl.when(c == 3)
    def _():
        settle(self_in.at[0], sem_self_recv.at[0])
        send_self(self_tile(1) + self_in[0].astype(jnp.float32), 2, 1, 2)

    subs = size // 16
    share_acc[...] = jnp.zeros_like(share_acc)
    groups = ring // 8

    def share_step(r, carry):
        settle(query_rows(r, across), sem_query.at[1, r])
        theirs = query_rows(r, across)
        remote(theirs, theirs, sem_query.at[4, r], sem_query.at[5, r], (beside, me)).start()
        target = lax.broadcasted_iota(jnp.int32, (ring * 16, 128), 0)
        codes = jnp.sum(
            jnp.where(note_row == r, notes[...], 0).reshape(groups, 8, 8, 128), axis=1
        )
        codes = jnp.sum(codes, axis=1)
        spread = jnp.concatenate(
            [
                (target == codes[g : g + 1, :]).astype(jnp.float32).astype(jnp.bfloat16)
                for g in range(groups)
            ],
            axis=1,
        )
        settle(shares.at[r, pl.ds(0, ring - 1)], sem_share_recv.at[r])
        for s in range(subs):
            part = shares[r, :, s * 16 : (s + 1) * 16, :].reshape(ring * 16, HEAD_DIM)
            share_acc[s] += dot_nn(spread, part)
        return carry

    lax.fori_loop(0, count, share_step, 0)
    for s in range(subs):
        totals[:, s * 16 : (s + 1) * 16, :] = (
            share_acc[s].reshape(ring, 16, HEAD_DIM).astype(jnp.bfloat16)
        )

    home = returned.at[
        aligned(own_block * size, size), columns(own_kind * half + c * HEAD_DIM, HEAD_DIM)
    ]

    @pl.when(c == source)
    def _():
        pltpu.make_async_copy(totals.at[me], home, sem_total.at[2]).start()

    @pl.when(c != source)
    def _():
        remote(totals.at[me], home, sem_total.at[0], sem_total.at[1], (source, me)).start()

    def send_total(step, carry):
        there = moved(step)
        remote(
            totals.at[there], home, sem_total.at[0], sem_total.at[1], (source, there)
        ).start()
        return carry

    lax.fori_loop(1, ring, send_total, 0)

    def add_self(slot):
        settle(self_in.at[slot], sem_self_recv.at[slot])
        return self_in[slot].astype(jnp.float32)

    own_rows = pl.ds(pl.multiple_of(c * rows, rows), rows)

    @pl.when(c == 0)
    def _():
        self_acc[own_rows, :] += add_self(0) + add_self(2)

    @pl.when(c == 1)
    def _():
        self_acc[own_rows, :] += add_self(2)

    @pl.when(c == 2)
    def _():
        self_acc[own_rows, :] += add_self(1)

    settle(notes.at[pl.ds(0, ring - 1)], sem_note.at[0])

    @pl.when(c == source)
    def _():
        settle(pieces_in.at[pl.ds(0, ring - 1)], sem_piece.at[0])

    @pl.when(c != source)
    def _():
        settle(pieces_in, sem_piece.at[0])

    @pl.when(c == 0)
    def _():
        send_tile(pkv, 0, 0, 2).wait_send()
        send_tile(pkv, 0, 1, 1).wait_send()

    @pl.when(c == 1)
    def _():
        send_tile(pkv, 1, 0, 3).wait_send()

    @pl.when(c == 2)
    def _():
        send_tile(pkv, 2, 0, 3).wait_send()
        send_tile(tile(0), 0, 1, 3).wait_send()

    @pl.when(c == 3)
    def _():
        send_tile(tile(1), 1, 0, 2).wait_send()

    @pl.when(c >= 1)
    def _():
        settle(self_out.at[0], sem_self_send.at[0])

    @pl.when(c == 3)
    def _():
        settle(self_out.at[1], sem_self_send.at[1])

    @pl.when(c >= 2)
    def _():
        settle(self_out.at[2], sem_self_send.at[2])

    for kind in range(2):
        settle(tree_part(kind, across), sem_tree.at[1, kind])
        theirs = tree_part(kind, across)
        remote(theirs, theirs, sem_tree.at[4, kind], sem_tree.at[5, kind], (beside, me)).start()
    for r in range(count):
        settle(picked.at[r, pl.ds(0, ring - 1)], sem_pick_send.at[r])
        settle(shares.at[r, pl.ds(0, ring - 1)], sem_share_send.at[r])
        for slot in (0, 2, 3, 4, 5, 6):
            settle(drq_v.at[r], sem_query.at[slot, r])
    for kind, values in ((0, dtree_k), (1, dtree_v)):
        for slot in (0, 2, 3, 4, 5, 6):
            settle(values, sem_tree.at[slot, kind])
    store_dpq.wait()

    @pl.when(c == source)
    def _():
        settle(totals.at[me], sem_total.at[2])
        settle(totals.at[pl.ds(0, ring - 1)], sem_total.at[0])
        settle(totals.at[pl.ds(0, ring - 1)], sem_total.at[1])

    @pl.when(c != source)
    def _():
        settle(totals, sem_total.at[0])
        settle(totals, sem_total.at[1])

    dpkv[...] = (self_acc[own_rows, :] + returned[...].astype(jnp.float32)).astype(jnp.bfloat16)


def body(
    prompt_q, prompt_kv, prompt_cot, resp_q, resp_kv, resp_cot, resp_prompt, tree_end, rewards
):
    ring = lax.axis_size("resp")
    rows, wide = prompt_q.shape[1:]
    kv_wide = prompt_kv.shape[2]
    count, tokens = resp_q.shape[:2]
    length = CTX * rows
    group = wide // (KV_HEADS * HEAD_DIM)
    width = group * HEAD_DIM
    size = 2 * length // ring
    bf16, f32, i32 = jnp.bfloat16, jnp.float32, jnp.int32
    any_space = pl.BlockSpec(memory_space=pl.ANY)
    scalars = pl.BlockSpec(memory_space=pltpu.SMEM)
    vector = pl.BlockSpec(memory_space=pltpu.VMEM)
    dma = pltpu.SemaphoreType.DMA
    dpq, dpkv, drq, drkv = pl.pallas_call(
        functools.partial(kernel, ring),
        out_shape=(
            jax.ShapeDtypeStruct((rows, wide), bf16),
            jax.ShapeDtypeStruct((rows, kv_wide), bf16),
            jax.ShapeDtypeStruct(resp_q.shape, bf16),
            jax.ShapeDtypeStruct(resp_kv.shape, bf16),
        ),
        in_specs=[scalars, scalars, vector] + [any_space] * 6,
        out_specs=(any_space, vector, any_space, any_space),
        scratch_shapes=[
            pltpu.VMEM((rows, wide), bf16),
            pltpu.VMEM((rows, wide), bf16),
            pltpu.VMEM((length, kv_wide), bf16),
            pltpu.VMEM((count, tokens, width), bf16),
            pltpu.VMEM((count, tokens, width), bf16),
            pltpu.VMEM((count, tokens, HEAD_DIM), bf16),
            pltpu.VMEM((count, tokens, HEAD_DIM), bf16),
            pltpu.VMEM((ring, 8, 128), i32),
            pltpu.VMEM((ring, 128), i32),
            pltpu.SMEM((ring, 128), i32),
            pltpu.VMEM((ring, size, HEAD_DIM), bf16),
            pltpu.VMEM((count, ring, size, HEAD_DIM), bf16),
            pltpu.VMEM((count, 2 * length, HEAD_DIM), bf16),
            pltpu.VMEM((length, 2 * rows), f32),
            pltpu.VMEM((length, kv_wide), f32),
            pltpu.VMEM((3, rows, kv_wide), bf16),
            pltpu.VMEM((3, rows, kv_wide), bf16),
            pltpu.VMEM((rows, wide), bf16),
            pltpu.VMEM((count, 2 * length, HEAD_DIM), bf16),
            pltpu.VMEM((count, ring, size, HEAD_DIM), bf16),
            pltpu.VMEM((size // 16, ring * 16, HEAD_DIM), f32),
            pltpu.VMEM((ring, size, HEAD_DIM), bf16),
            pltpu.VMEM((rows, kv_wide), bf16),
            pltpu.VMEM((count, tokens, width), bf16),
            pltpu.VMEM((count, tokens, HEAD_DIM), bf16),
            pltpu.VMEM((count, tokens, HEAD_DIM), bf16),
            dma((8,)),
            dma((3,)),
            dma((3,)),
            dma((2,)),
            dma((CTX,)),
            dma((count,)),
            dma((count,)),
            dma((3,)),
            dma((3,)),
            dma((count,)),
            dma((count,)),
            dma((7, count)),
            dma((7, 2)),
            dma((3,)),
        ],
        compiler_params=pltpu.CompilerParams(
            collective_id=0, has_side_effects=True, vmem_limit_bytes=56 * 1024 * 1024
        ),
        name="attention_gradients",
    )(
        resp_prompt,
        rewards,
        tree_end,
        prompt_q[0],
        prompt_kv[0],
        prompt_cot[0],
        resp_q,
        resp_kv,
        resp_cot,
    )
    return (dpq[None], dpkv[None], drq, drkv)


def solution(mesh):
    in_specs = (
        P("resp", "ctx", None),
        P("resp", "ctx", None),
        P("resp", "ctx", None),
        P("resp", None, None),
        P("resp", None, None),
        P("resp", None, None),
        P("resp", None),
        P("resp", None),
        P("resp"),
    )
    out_specs = (
        P("resp", "ctx", None),
        P("resp", "ctx", None),
        P("resp", None, None),
        P("resp", None, None),
    )
    return jax.shard_map(body, mesh=mesh, in_specs=in_specs, out_specs=out_specs, check_vma=False)
```

```python
import functools
import math

import jax
import jax.numpy as jnp
from jax import lax
from jax.experimental import pallas as pl
from jax.experimental.pallas import tpu as pltpu
from jax.sharding import PartitionSpec as P

MESH = pl.DeviceIdType.MESH
KV_HEADS = 4
HEAD_DIM = 128
CTX = 4
ROUTE_ROW = 4
REWARD_ROW = 5
PARTS = 2


def dot_nt(a, b):
    return lax.dot_general(a, b, (((1,), (1,)), ((), ())), preferred_element_type=jnp.float32)


def dot_tn(a, b):
    return lax.dot_general(a, b, (((0,), (0,)), ((), ())), preferred_element_type=jnp.float32)


def dot_nn(a, b):
    return lax.dot_general(a, b, (((1,), (0,)), ((), ())), preferred_element_type=jnp.float32)


def aligned(start, size):
    return pl.ds(pl.multiple_of(start, 16), size)


def columns(start, size):
    return pl.ds(pl.multiple_of(start, 128), size)


def attention_grads(queries, cotangent, pieces, scale):
    to_power = scale * math.log2(math.e)
    scores = []
    for keys, values, adjust in pieces:
        part = dot_nt(keys, queries) * to_power
        scores.append(part if adjust is None else adjust(part))
    highest = functools.reduce(
        jnp.maximum, [jnp.max(part, axis=0, keepdims=True) for part in scores]
    )
    powers = [jnp.exp2(part - highest) for part in scores]
    total = functools.reduce(jnp.add, [jnp.sum(part, axis=0, keepdims=True) for part in powers])
    inverse = 1.0 / total
    grad_probs = [dot_nt(values, cotangent) for keys, values, adjust in pieces]
    delta = inverse * functools.reduce(
        jnp.add,
        [jnp.sum(a * b, axis=0, keepdims=True) for a, b in zip(powers, grad_probs)],
    )
    grad_query = None
    grads = []
    for (keys, values, adjust), power, grad_prob in zip(pieces, powers, grad_probs):
        weight = power * inverse
        narrow = weight.astype(jnp.bfloat16)
        grad_score = (weight * (grad_prob - delta)).astype(jnp.bfloat16)
        grad_values = dot_nn(narrow, cotangent)
        grad_keys = dot_nn(grad_score, queries)
        term = dot_tn(keys, grad_score)
        grad_query = term if grad_query is None else grad_query + term
        grads.append((grad_keys, grad_values))
    return grad_query, grads


def cut(ring):
    halves = 2 if ring >= 16 else 1
    return halves, ring // halves


def kernel(
    ring,
    routes_in,
    rewards_in,
    tree_in,
    pq,
    pkv,
    pcot,
    rq,
    rkv,
    rcot,
    dpq,
    dpkv,
    drq,
    drkv,
    pq_v,
    pcot_v,
    tiles,
    rq_v,
    rcot_v,
    tree_k,
    tree_v,
    notes,
    picks_v,
    picks,
    pieces_in,
    picked,
    chosen,
    bias,
    self_acc,
    self_out,
    self_in,
    grads,
    shares,
    share_acc,
    totals,
    returned,
    sem_load,
    sem_note,
    sem_piece,
    sem_tile_send,
    sem_tile_recv,
    sem_pick_send,
    sem_pick_recv,
    sem_self_send,
    sem_self_recv,
    sem_share_send,
    sem_share_recv,
    sem_query,
    sem_tree,
    sem_total,
):
    scale = 1.0 / math.sqrt(HEAD_DIM)
    c = lax.axis_index("ctx")
    me = lax.axis_index("resp")
    rows = pq.shape[0]
    length = CTX * rows
    count, tokens = rq.shape[0], rq.shape[1]
    group = pq.shape[1] // (KV_HEADS * HEAD_DIM)
    width = group * HEAD_DIM
    half = KV_HEADS * HEAD_DIM
    halves, plane = cut(ring)
    size = 2 * length // plane
    blocks = rows // size
    my_half = me // plane
    my_place = lax.rem(me, plane)
    source = lax.rem(my_place, plane // 2) // blocks
    own_block = lax.rem(my_place, blocks)
    own_kind = my_place // (plane // 2)
    beside = c + 1 - 2 * lax.rem(c, 2)
    across = lax.rem(c + 2, CTX)
    x_size = 4
    y_size = plane // x_size

    def moved(step):
        x = lax.rem(lax.rem(me, x_size) + lax.rem(step, x_size), x_size)
        y = lax.rem(lax.rem(me // x_size, y_size) + lax.rem(step // x_size, y_size), y_size)
        z = lax.rem(my_half + step // plane, halves)
        return z * plane + y * x_size + x

    def remote(src, dst, send, recv, where):
        return pltpu.make_async_remote_copy(
            src_ref=src,
            dst_ref=dst,
            send_sem=send,
            recv_sem=recv,
            device_id=where,
            device_id_type=MESH,
        )

    def settle(ref, sem):
        pltpu.make_async_copy(ref, ref, sem).wait()

    own_tile = pltpu.make_async_copy(pkv, tiles.at[aligned(c * rows, rows)], sem_load.at[0])
    own_tree_k = pltpu.make_async_copy(
        rkv.at[:, :, columns(c * HEAD_DIM, HEAD_DIM)], tree_k, sem_load.at[1]
    )
    own_tree_v = pltpu.make_async_copy(
        rkv.at[:, :, columns(half + c * HEAD_DIM, HEAD_DIM)], tree_v, sem_load.at[2]
    )

    barrier = pltpu.get_barrier_semaphore()

    def greet(step, carry):
        there = (lax.rem(c + step // ring, CTX), lax.rem(me + lax.rem(step, ring), ring))
        pl.semaphore_signal(barrier, inc=1, device_id=there, device_id_type=MESH)
        return carry

    lax.fori_loop(1, CTX * ring, greet, 0)

    own_tile.start()
    own_tree_k.start()
    own_tree_v.start()

    def load_prompt_head(head, carry):
        source_columns = columns(head * HEAD_DIM, HEAD_DIM)
        place = aligned(head * rows, rows)
        pltpu.make_async_copy(pq.at[:, source_columns], pq_v.at[place], sem_load.at[3]).start()
        pltpu.make_async_copy(pcot.at[:, source_columns], pcot_v.at[place], sem_load.at[4]).start()
        return carry

    def load_response_head(head, carry):
        source_columns = columns(c * width + head * HEAD_DIM, HEAD_DIM)
        place = aligned(head * tokens, tokens)
        pltpu.make_async_copy(
            rq.at[:, :, source_columns], rq_v.at[:, place], sem_load.at[5]
        ).start()
        pltpu.make_async_copy(
            rcot.at[:, :, source_columns], rcot_v.at[:, place], sem_load.at[6]
        ).start()
        return carry

    lax.fori_loop(0, KV_HEADS * group, load_prompt_head, 0)
    lax.fori_loop(0, group, load_response_head, 0)

    row = lax.broadcasted_iota(jnp.int32, (8, 128), 0)
    lane = lax.broadcasted_iota(jnp.int32, (8, 128), 1)
    note = jnp.zeros((8, 128), jnp.int32)
    inside = lane // 16 == lax.rem(me, 8)
    for r in range(count):
        route = routes_in[r]
        note = jnp.where((row == r) & inside, route * 16 + lane % 16, note)
        note = jnp.where((row == ROUTE_ROW) & (lane == r), route, note)
        note = jnp.where((row == REWARD_ROW) & (lane == r), rewards_in[r], note)
    notes[me] = note

    pl.semaphore_wait(barrier, CTX * ring - 1)

    def send_note(step, carry):
        there = moved(step)
        remote(notes.at[me], notes.at[me], sem_note.at[0], sem_note.at[1], (c, there)).start()
        return carry

    lax.fori_loop(1, ring, send_note, 0)

    def send_piece(step, carry):
        head = lax.rem(c + step, KV_HEADS)
        part = lax.rem(step // KV_HEADS + my_place, 2 * blocks)
        kind = part // blocks
        block = lax.rem(part, blocks)
        there_half = lax.rem(my_half + step // (KV_HEADS * 2 * blocks), halves)
        there = there_half * plane + kind * (plane // 2) + c * blocks + block
        piece = pkv.at[
            aligned(block * size, size), columns(kind * half + head * HEAD_DIM, HEAD_DIM)
        ]
        here = (head == c) & (there == me)

        @pl.when(here)
        def _():
            pltpu.make_async_copy(piece, pieces_in.at[me], sem_piece.at[2]).start()

        @pl.when(jnp.logical_not(here))
        def _():
            remote(
                piece, pieces_in.at[me], sem_piece.at[0], sem_piece.at[1], (head, there)
            ).start()

        return carry

    piece_count = halves * KV_HEADS * 2 * blocks
    lax.fori_loop(0, piece_count, send_piece, 0)

    def tile(index):
        return tiles.at[pl.ds(index * rows, rows)]

    def send_tile(src, index, slot, where):
        return remote(src, tile(index), sem_tile_send.at[slot], sem_tile_recv.at[index], (where, me))

    @pl.when(c == 0)
    def _():
        send_tile(pkv, 0, 0, 2).start()
        send_tile(pkv, 0, 1, 1).start()

    @pl.when(c == 1)
    def _():
        send_tile(pkv, 1, 0, 3).start()

    @pl.when(c == 2)
    def _():
        send_tile(pkv, 2, 0, 3).start()

    for index in range(1, CTX):

        @pl.when(c < index)
        def _():
            tiles[index * rows : (index + 1) * rows, :] = jnp.zeros((rows, 2 * half), jnp.bfloat16)

    stack = min(4, group)
    position = lax.broadcasted_iota(jnp.int32, (length, rows), 0)
    query = lax.broadcasted_iota(jnp.int32, (length, rows), 1) + c * rows
    allowed_here = jnp.where(position <= query, 0.0, -jnp.inf)
    for index in range(stack):
        bias[:, index * rows : (index + 1) * rows] = allowed_here
    self_acc[...] = jnp.zeros_like(self_acc)
    share_acc[...] = jnp.zeros_like(share_acc)

    settle(notes.at[pl.ds(0, ring - 1)], sem_note.at[1])
    every = notes[...]
    note_row = lax.broadcasted_iota(jnp.int32, every.shape, 1)
    routes = jnp.sum(jnp.where(note_row == ROUTE_ROW, every, 0), axis=1)
    rewards = jnp.sum(jnp.where(note_row == REWARD_ROW, every, 0), axis=1).astype(jnp.float32)
    picks_v[...] = routes
    to_scalars = pltpu.make_async_copy(picks_v, picks, sem_note.at[2])
    to_scalars.start()
    to_scalars.wait()

    @pl.when(c == source)
    def _():
        settle(pieces_in.at[me], sem_piece.at[2])
        settle(pieces_in.at[pl.ds(0, ring - 1)], sem_piece.at[1])

    @pl.when(c != source)
    def _():
        settle(pieces_in, sem_piece.at[1])

    def send_pick(step, carry):
        r = step // (plane - 1)
        there = moved(lax.rem(step, plane - 1) + 1)
        there_place = lax.rem(there, plane)
        picked[r, there_place] = pieces_in[picks[there, r]]
        remote(
            picked.at[r, there_place],
            chosen.at[r, aligned(my_place * size, size)],
            sem_pick_send.at[r],
            sem_pick_recv.at[r],
            (c, there),
        ).start()
        return carry

    lax.fori_loop(0, count * (plane - 1), send_pick, 0)
    for r in range(count):
        chosen[r, aligned(my_place * size, size), :] = pieces_in[picks[me, r]]

    @pl.when(c == 2)
    def _():
        settle(tile(0), sem_tile_recv.at[0])
        send_tile(tile(0), 0, 1, 3).start()
        settle(tile(1), sem_tile_recv.at[1])

    @pl.when(c == 3)
    def _():
        settle(tile(1), sem_tile_recv.at[1])
        send_tile(tile(1), 1, 0, 2).start()
        settle(tile(0), sem_tile_recv.at[0])
        settle(tile(2), sem_tile_recv.at[2])

    @pl.when(c == 1)
    def _():
        settle(tile(0), sem_tile_recv.at[0])

    own_tile.wait()
    own_tree_k.wait()
    own_tree_v.wait()
    settle(pq_v, sem_load.at[3])
    settle(pcot_v, sem_load.at[4])
    settle(rq_v, sem_load.at[5])
    settle(rcot_v, sem_load.at[6])

    parts = group // stack
    together = stack * rows

    def prompt_step(step, carry):
        head = step // parts
        key_columns = columns(head * HEAD_DIM, HEAD_DIM)
        value_columns = columns(half + head * HEAD_DIM, HEAD_DIM)
        place = aligned(step * together, together)
        grad_query, ((grad_keys, grad_values),) = attention_grads(
            pq_v[place, :],
            pcot_v[place, :],
            [(tiles[:, key_columns], tiles[:, value_columns], lambda part: part + bias[...])],
            scale,
        )
        self_acc[:, key_columns] += grad_keys * scale
        self_acc[:, value_columns] += grad_values
        turned = jnp.transpose((grad_query * scale).astype(jnp.bfloat16))
        for index in range(stack):
            dpq[:, columns((step * stack + index) * HEAD_DIM, HEAD_DIM)] = turned[
                index * rows : (index + 1) * rows
            ]
        return carry

    part_width = half // PARTS

    def self_tile(index, part):
        here = slice(index * rows, (index + 1) * rows)
        keys = slice(part * part_width, (part + 1) * part_width)
        values = slice(half + part * part_width, half + (part + 1) * part_width)
        return jnp.concatenate([self_acc[here, keys], self_acc[here, values]], axis=1)

    def send_self(values, part, slot, there, there_slot):
        self_out[part, slot] = values.astype(jnp.bfloat16)
        remote(
            self_out.at[part, slot],
            self_in.at[part, there_slot],
            sem_self_send.at[part, slot],
            sem_self_recv.at[part, there_slot],
            (there, me),
        ).start()

    def prompt_part(part):
        steps = KV_HEADS * parts // PARTS
        lax.fori_loop(part * steps, (part + 1) * steps, prompt_step, 0)

        @pl.when(c == 1)
        def _():
            send_self(self_tile(0, part), part, 0, 0, 0)

        @pl.when(c == 2)
        def _():
            send_self(self_tile(1, part), part, 0, 3, 0)

        @pl.when(c == 3)
        def _():
            send_self(self_tile(0, part), part, 0, 2, 0)
            send_self(self_tile(2, part), part, 1, 2, 1)

    def cross_self(part):
        for core, index in ((2, 0), (3, 1)):

            @pl.when(c == core)
            def _():
                settle(self_in.at[part, 0], sem_self_recv.at[part, 0])
                theirs = self_in[part, 0].astype(jnp.float32)
                send_self(self_tile(index, part) + theirs, part, 2, index, 2)

    prompt_part(0)

    note_lane = lax.broadcasted_iota(jnp.int32, routes.shape, 1)
    for r in range(count):
        same = ((routes == routes_in[r]) & (note_lane < count)).astype(jnp.float32)

        def summed(values):
            return jnp.sum(jnp.sum(values, axis=1, keepdims=True), axis=0, keepdims=True)

        number = summed(same)
        reward_sum = summed(same * rewards)
        reward_square = summed(same * rewards * rewards)
        variance = reward_square * number - reward_sum * reward_sum
        spread = jnp.sqrt(jnp.maximum(variance, number * number)) / number
        own_reward = jnp.full((1, 1), rewards_in[r], jnp.int32).astype(jnp.float32)
        advantage = (own_reward - reward_sum / number) / spread
        rcot_v[r] = (advantage * rcot_v[r].astype(jnp.float32)).astype(jnp.bfloat16)

    key_place = lax.broadcasted_iota(jnp.int32, (tokens, group * tokens), 0)
    query_place = lax.broadcasted_iota(jnp.int32, (tokens, group * tokens), 1) % tokens
    square_row = lax.broadcasted_iota(jnp.int32, (tokens, tokens), 0)
    square_column = lax.broadcasted_iota(jnp.int32, (tokens, tokens), 1)

    def query_rows(r, owner):
        return drq.at[r, :, columns(owner * width, width)]

    def response_step(r, carry):
        settle(chosen.at[r, pl.ds(0, (plane - 1) * size)], sem_pick_recv.at[r])
        ends = tree_in[pl.ds(r, 1), :]
        ends = jnp.sum(
            jnp.where(square_row == square_column, ends, 0), axis=1, keepdims=True
        )
        allowed = (key_place <= query_place) & (query_place < ends)
        grad_query, (prompt_terms, tree_terms) = attention_grads(
            rq_v[r],
            rcot_v[r],
            [
                (chosen[r, :length, :], chosen[r, length:, :], None),
                (tree_k[r], tree_v[r], lambda part: jnp.where(allowed, part, -jnp.inf)),
            ],
            scale,
        )
        grads[r, :length, :] = (prompt_terms[0] * scale).astype(jnp.bfloat16)
        grads[r, length:, :] = prompt_terms[1].astype(jnp.bfloat16)
        drkv[r, :, columns(c * HEAD_DIM, HEAD_DIM)] = (tree_terms[0] * scale).astype(jnp.bfloat16)
        drkv[r, :, columns(half + c * HEAD_DIM, HEAD_DIM)] = tree_terms[1].astype(jnp.bfloat16)
        turned = jnp.transpose((grad_query * scale).astype(jnp.bfloat16))
        drq[r, :, columns(c * width, width)] = jnp.concatenate(
            [turned[g * tokens : (g + 1) * tokens] for g in range(group)], axis=1
        )

        def send_share(step, inner):
            there = moved(step)
            remote(
                grads.at[r, aligned(lax.rem(there, plane) * size, size)],
                shares.at[r, my_place],
                sem_share_send.at[r],
                sem_share_recv.at[r],
                (c, there),
            ).start()
            return inner

        mine = query_rows(r, c)
        remote(mine, mine, sem_query.at[0, r], sem_query.at[1, r], (across, me)).start()
        lax.fori_loop(1, plane, send_share, 0)
        remote(mine, mine, sem_query.at[2, r], sem_query.at[3, r], (beside, me)).start()
        shares[r, my_place] = grads[r, aligned(my_place * size, size), :]
        return carry

    lax.fori_loop(0, count, response_step, 0)

    def tree_part(kind, owner):
        return drkv.at[:, :, columns(kind * half + owner * HEAD_DIM, HEAD_DIM)]

    for kind in range(2):
        mine = tree_part(kind, c)
        remote(mine, mine, sem_tree.at[0, kind], sem_tree.at[1, kind], (across, me)).start()
        remote(mine, mine, sem_tree.at[2, kind], sem_tree.at[3, kind], (beside, me)).start()

    cross_self(0)
    for part in range(1, PARTS):
        prompt_part(part)

    subs = size // 16
    groups = plane // 8

    def share_step(r, carry):
        target = lax.broadcasted_iota(jnp.int32, (ring * 16, 128), 0)
        place = lax.broadcasted_iota(jnp.int32, (8, 8, 128), 1)
        spread = []
        for index in range(groups):
            near = notes[pl.ds(my_half * plane + index * 8, 8)]
            codes = jnp.sum(jnp.where(place == r, near, 0), axis=0)
            codes = jnp.sum(codes, axis=0, keepdims=True)
            spread.append((target == codes).astype(jnp.float32).astype(jnp.bfloat16))
        spread = jnp.concatenate(spread, axis=1)
        settle(shares.at[r, pl.ds(0, plane - 1)], sem_share_recv.at[r])
        for s in range(subs):
            part = shares[r, :, s * 16 : (s + 1) * 16, :].reshape(plane * 16, HEAD_DIM)
            share_acc[s] += dot_nn(spread, part)
        theirs = query_rows(r, across)
        settle(theirs, sem_query.at[1, r])
        remote(theirs, theirs, sem_query.at[4, r], sem_query.at[5, r], (beside, me)).start()
        return carry

    def share_steps(first, last):
        lax.fori_loop(first, last, share_step, 0)

    for part in range(1, PARTS):
        cross_self(part)
    share_steps(0, count)
    for s in range(subs):
        totals[:, s * 16 : (s + 1) * 16, :] = (
            share_acc[s].reshape(ring, 16, HEAD_DIM).astype(jnp.bfloat16)
        )

    home = returned.at[
        my_half,
        aligned(own_block * size, size),
        columns(own_kind * half + c * HEAD_DIM, HEAD_DIM),
    ]

    @pl.when(c == source)
    def _():
        pltpu.make_async_copy(totals.at[me], home, sem_total.at[2]).start()

    @pl.when(c != source)
    def _():
        remote(totals.at[me], home, sem_total.at[0], sem_total.at[1], (source, me)).start()

    def send_total(step, carry):
        there = moved(step)
        remote(
            totals.at[there], home, sem_total.at[0], sem_total.at[1], (source, there)
        ).start()
        return carry

    lax.fori_loop(1, ring, send_total, 0)

    for kind in range(2):
        theirs = tree_part(kind, across)
        settle(theirs, sem_tree.at[1, kind])
        remote(theirs, theirs, sem_tree.at[4, kind], sem_tree.at[5, kind], (beside, me)).start()

    def add_self(part, slot):
        settle(self_in.at[part, slot], sem_self_recv.at[part, slot])
        return self_in[part, slot].astype(jnp.float32)

    own_rows = pl.ds(pl.multiple_of(c * rows, rows), rows)
    for part in range(PARTS):
        keys = slice(part * part_width, (part + 1) * part_width)
        values = slice(half + part * part_width, half + (part + 1) * part_width)

        def add(more):
            self_acc[own_rows, keys] += more[:, :part_width]
            self_acc[own_rows, values] += more[:, part_width:]

        @pl.when(c == 0)
        def _():
            add(add_self(part, 0) + add_self(part, 2))

        @pl.when(c == 1)
        def _():
            add(add_self(part, 2))

        @pl.when(c == 2)
        def _():
            add(add_self(part, 1))

        @pl.when(c >= 1)
        def _():
            settle(self_out.at[part, 0], sem_self_send.at[part, 0])

        @pl.when(c == 3)
        def _():
            settle(self_out.at[part, 1], sem_self_send.at[part, 1])

        @pl.when(c >= 2)
        def _():
            settle(self_out.at[part, 2], sem_self_send.at[part, 2])

    settle(notes.at[pl.ds(0, ring - 1)], sem_note.at[0])

    @pl.when(c == source)
    def _():
        settle(pieces_in.at[pl.ds(0, piece_count - 1)], sem_piece.at[0])

    @pl.when(c != source)
    def _():
        settle(pieces_in.at[pl.ds(0, piece_count)], sem_piece.at[0])

    @pl.when(c == 0)
    def _():
        send_tile(pkv, 0, 0, 2).wait_send()
        send_tile(pkv, 0, 1, 1).wait_send()

    @pl.when(c == 1)
    def _():
        send_tile(pkv, 1, 0, 3).wait_send()

    @pl.when(c == 2)
    def _():
        send_tile(pkv, 2, 0, 3).wait_send()
        send_tile(tile(0), 0, 1, 3).wait_send()

    @pl.when(c == 3)
    def _():
        send_tile(tile(1), 1, 0, 2).wait_send()

    for r in range(count):
        settle(picked.at[r, pl.ds(0, plane - 1)], sem_pick_send.at[r])
        settle(shares.at[r, pl.ds(0, plane - 1)], sem_share_send.at[r])
        for slot in (0, 2, 3, 4, 5):
            settle(query_rows(r, c), sem_query.at[slot, r])
    for kind in range(2):
        for slot in (0, 2, 3, 4, 5):
            settle(tree_part(kind, c), sem_tree.at[slot, kind])

    @pl.when(c == source)
    def _():
        settle(totals.at[me], sem_total.at[2])
        settle(totals.at[pl.ds(0, ring - 1)], sem_total.at[0])

    @pl.when(c != source)
    def _():
        settle(totals, sem_total.at[0])

    others = halves * KV_HEADS * 2 * blocks

    @pl.when(c == source)
    def _():
        settle(totals.at[pl.ds(0, others - 1)], sem_total.at[1])

    @pl.when(c != source)
    def _():
        settle(totals.at[pl.ds(0, others)], sem_total.at[1])

    dpkv[...] = (
        self_acc[own_rows, :]
        + functools.reduce(jnp.add, [returned[z].astype(jnp.float32) for z in range(halves)])
    ).astype(jnp.bfloat16)


def body(
    prompt_q, prompt_kv, prompt_cot, resp_q, resp_kv, resp_cot, resp_prompt, tree_end, rewards
):
    ring = lax.axis_size("resp")
    rows, wide = prompt_q.shape[1:]
    kv_wide = prompt_kv.shape[2]
    count, tokens = resp_q.shape[:2]
    length = CTX * rows
    group = wide // (KV_HEADS * HEAD_DIM)
    width = group * HEAD_DIM
    halves, plane = cut(ring)
    size = 2 * length // plane
    bf16, f32, i32 = jnp.bfloat16, jnp.float32, jnp.int32
    any_space = pl.BlockSpec(memory_space=pl.ANY)
    scalars = pl.BlockSpec(memory_space=pltpu.SMEM)
    vector = pl.BlockSpec(memory_space=pltpu.VMEM)
    dma = pltpu.SemaphoreType.DMA
    dpq, dpkv, drq, drkv = pl.pallas_call(
        functools.partial(kernel, ring),
        out_shape=(
            pltpu.VMEM((rows, wide), bf16),
            pltpu.VMEM((rows, kv_wide), bf16),
            pltpu.VMEM(resp_q.shape, bf16),
            pltpu.VMEM(resp_kv.shape, bf16),
        ),
        in_specs=[scalars, scalars, vector] + [any_space] * 6,
        out_specs=(vector,) * 4,
        scratch_shapes=[
            pltpu.VMEM((wide // HEAD_DIM * rows, HEAD_DIM), bf16),
            pltpu.VMEM((wide // HEAD_DIM * rows, HEAD_DIM), bf16),
            pltpu.VMEM((length, kv_wide), bf16),
            pltpu.VMEM((count, group * tokens, HEAD_DIM), bf16),
            pltpu.VMEM((count, group * tokens, HEAD_DIM), bf16),
            pltpu.VMEM((count, tokens, HEAD_DIM), bf16),
            pltpu.VMEM((count, tokens, HEAD_DIM), bf16),
            pltpu.VMEM((ring, 8, 128), i32),
            pltpu.VMEM((ring, 128), i32),
            pltpu.SMEM((ring, 128), i32),
            pltpu.VMEM((ring, size, HEAD_DIM), bf16),
            pltpu.VMEM((count, plane, size, HEAD_DIM), bf16),
            pltpu.VMEM((count, 2 * length, HEAD_DIM), bf16),
            pltpu.VMEM((length, min(4, group) * rows), f32),
            pltpu.VMEM((length, kv_wide), f32),
            pltpu.VMEM((PARTS, 3, rows, kv_wide // PARTS), bf16),
            pltpu.VMEM((PARTS, 3, rows, kv_wide // PARTS), bf16),
            pltpu.VMEM((count, 2 * length, HEAD_DIM), bf16),
            pltpu.VMEM((count, plane, size, HEAD_DIM), bf16),
            pltpu.VMEM((size // 16, ring * 16, HEAD_DIM), f32),
            pltpu.VMEM((ring, size, HEAD_DIM), bf16),
            pltpu.VMEM((halves, rows, kv_wide), bf16),
            dma((7,)),
            dma((3,)),
            dma((3,)),
            dma((2,)),
            dma((CTX,)),
            dma((count,)),
            dma((count,)),
            dma((PARTS, 3)),
            dma((PARTS, 3)),
            dma((count,)),
            dma((count,)),
            dma((6, count)),
            dma((6, 2)),
            dma((3,)),
        ],
        compiler_params=pltpu.CompilerParams(
            collective_id=0, has_side_effects=True, vmem_limit_bytes=52 * 1024 * 1024
        ),
        name="attention_gradients",
    )(
        resp_prompt[:, 0],
        rewards,
        tree_end,
        prompt_q[0],
        prompt_kv[0],
        prompt_cot[0],
        resp_q,
        resp_kv,
        resp_cot,
    )
    return (dpq[None], dpkv[None], drq, drkv)


def solution(mesh):
    in_specs = (
        P("resp", "ctx", None),
        P("resp", "ctx", None),
        P("resp", "ctx", None),
        P("resp", None, None),
        P("resp", None, None),
        P("resp", None, None),
        P("resp", None),
        P("resp", None),
        P("resp"),
    )
    out_specs = (
        P("resp", "ctx", None),
        P("resp", "ctx", None),
        P("resp", None, None),
        P("resp", None, None),
    )
    return jax.shard_map(body, mesh=mesh, in_specs=in_specs, out_specs=out_specs, check_vma=False)
```

```python
import functools
import math

import jax
import jax.numpy as jnp
from jax import lax
from jax.experimental import pallas as pl
from jax.experimental.pallas import tpu as pltpu
from jax.sharding import PartitionSpec as P

MESH = pl.DeviceIdType.MESH
KV_HEADS = 4
HEAD_DIM = 128
CTX = 4
ROUTE_ROW = 4
REWARD_ROW = 5
PARTS = 2


def dot_nt(a, b):
    return lax.dot_general(a, b, (((1,), (1,)), ((), ())), preferred_element_type=jnp.float32)


def dot_tn(a, b):
    return lax.dot_general(a, b, (((0,), (0,)), ((), ())), preferred_element_type=jnp.float32)


def dot_nn(a, b):
    return lax.dot_general(a, b, (((1,), (0,)), ((), ())), preferred_element_type=jnp.float32)


def aligned(start, size):
    return pl.ds(pl.multiple_of(start, 16), size)


def columns(start, size):
    return pl.ds(pl.multiple_of(start, 128), size)


def attention_grads(queries, cotangent, pieces, scale):
    to_power = scale * math.log2(math.e)
    scores = []
    for keys, values, adjust in pieces:
        part = dot_nt(keys, queries) * to_power
        scores.append(part if adjust is None else adjust(part))
    highest = functools.reduce(
        jnp.maximum, [jnp.max(part, axis=0, keepdims=True) for part in scores]
    )
    powers = [jnp.exp2(part - highest) for part in scores]
    total = functools.reduce(jnp.add, [jnp.sum(part, axis=0, keepdims=True) for part in powers])
    inverse = 1.0 / total
    grad_probs = [dot_nt(values, cotangent) for keys, values, adjust in pieces]
    delta = inverse * functools.reduce(
        jnp.add,
        [jnp.sum(a * b, axis=0, keepdims=True) for a, b in zip(powers, grad_probs)],
    )
    grad_query = None
    grads = []
    for (keys, values, adjust), power, grad_prob in zip(pieces, powers, grad_probs):
        weight = power * inverse
        narrow = weight.astype(jnp.bfloat16)
        grad_score = (weight * (grad_prob - delta)).astype(jnp.bfloat16)
        grad_values = dot_nn(narrow, cotangent)
        grad_keys = dot_nn(grad_score, queries)
        term = dot_tn(keys, grad_score)
        grad_query = term if grad_query is None else grad_query + term
        grads.append((grad_keys, grad_values))
    return grad_query, grads


def cut(ring):
    halves = 2 if ring >= 16 else 1
    return halves, ring // halves


def place_of(blocks, kind, ctx, block, head, z):
    if blocks != 2:
        return (kind * CTX + ctx) * blocks + block
    high, low = head // 2, head % 2
    y_high = lax.rem(ctx % 2 + high, 2)
    y_low = lax.rem(ctx // 2 + high, 2)
    x_high = lax.rem(kind + high + low + z, 2)
    x_low = lax.rem(block + low, 2)
    return ((y_high * 2 + y_low) * 2 + x_high) * 2 + x_low


def held_at(blocks, place, head, z):
    if blocks != 2:
        return place // (CTX * blocks), lax.rem(place // blocks, CTX), lax.rem(place, blocks)
    high, low = head // 2, head % 2
    ctx = lax.rem(place // 8 + high, 2) + 2 * lax.rem(lax.rem(place // 4, 2) + high, 2)
    kind = lax.rem(lax.rem(place // 2, 2) + high + low + z, 2)
    return kind, ctx, lax.rem(lax.rem(place, 2) + low, 2)


def kernel(
    ring,
    routes_in,
    rewards_in,
    tree_in,
    pq,
    pkv,
    pcot,
    rq,
    rkv,
    rcot,
    dpq,
    dpkv,
    drq,
    drkv,
    pq_v,
    pcot_v,
    tiles,
    own_columns,
    rq_v,
    rcot_v,
    tree_k,
    tree_v,
    notes,
    picks_v,
    picks,
    pieces_in,
    picked,
    chosen,
    bias,
    self_acc,
    self_out,
    self_in,
    grads,
    shares,
    share_acc,
    totals,
    returned,
    sem_load,
    sem_note,
    sem_piece,
    sem_tile_send,
    sem_tile_recv,
    sem_pick_send,
    sem_pick_recv,
    sem_self_send,
    sem_self_recv,
    sem_share_send,
    sem_share_recv,
    sem_query,
    sem_tree,
    sem_total,
):
    scale = 1.0 / math.sqrt(HEAD_DIM)
    c = lax.axis_index("ctx")
    me = lax.axis_index("resp")
    rows = pq.shape[0]
    length = CTX * rows
    count, tokens = rq.shape[0], rq.shape[1]
    group = pq.shape[1] // (KV_HEADS * HEAD_DIM)
    width = group * HEAD_DIM
    half = KV_HEADS * HEAD_DIM
    halves, plane = cut(ring)
    size = 2 * length // plane
    blocks = rows // size
    my_half = me // plane
    my_place = lax.rem(me, plane)
    own_kind, source, own_block = held_at(blocks, my_place, c, my_half)

    def position(place):
        kind, ctx, block = held_at(blocks, place, c, my_half)
        return (kind * CTX + ctx) * blocks + block

    my_position = position(my_place)
    beside = c + 1 - 2 * lax.rem(c, 2)
    across = lax.rem(c + 2, CTX)
    x_size = 4
    y_size = plane // x_size

    def moved(step):
        x = lax.rem(lax.rem(me, x_size) + lax.rem(step, x_size), x_size)
        y = lax.rem(lax.rem(me // x_size, y_size) + lax.rem(step // x_size, y_size), y_size)
        z = lax.rem(my_half + step // plane, halves)
        return z * plane + y * x_size + x

    def remote(src, dst, send, recv, where):
        return pltpu.make_async_remote_copy(
            src_ref=src,
            dst_ref=dst,
            send_sem=send,
            recv_sem=recv,
            device_id=where,
            device_id_type=MESH,
        )

    def settle(ref, sem):
        pltpu.make_async_copy(ref, ref, sem).wait()

    own_tile = pltpu.make_async_copy(pkv, tiles.at[aligned(c * rows, rows)], sem_load.at[0])
    own_tree_k = pltpu.make_async_copy(
        rkv.at[:, :, columns(c * HEAD_DIM, HEAD_DIM)], tree_k, sem_load.at[1]
    )
    own_tree_v = pltpu.make_async_copy(
        rkv.at[:, :, columns(half + c * HEAD_DIM, HEAD_DIM)], tree_v, sem_load.at[2]
    )

    barrier = pltpu.get_barrier_semaphore()

    def greet(step, carry):
        there = (lax.rem(c + step // ring, CTX), lax.rem(me + lax.rem(step, ring), ring))
        pl.semaphore_signal(barrier, inc=1, device_id=there, device_id_type=MESH)
        return carry

    lax.fori_loop(1, CTX * ring, greet, 0)

    own_tile.start()
    own_tree_k.start()
    own_tree_v.start()

    def load_prompt_head(head, carry):
        source_columns = columns(head * HEAD_DIM, HEAD_DIM)
        place = aligned(head * rows, rows)
        pltpu.make_async_copy(pq.at[:, source_columns], pq_v.at[place], sem_load.at[3]).start()
        pltpu.make_async_copy(pcot.at[:, source_columns], pcot_v.at[place], sem_load.at[4]).start()
        return carry

    def load_response_head(head, carry):
        source_columns = columns(c * width + head * HEAD_DIM, HEAD_DIM)
        place = aligned(head * tokens, tokens)
        pltpu.make_async_copy(
            rq.at[:, :, source_columns], rq_v.at[:, place], sem_load.at[5]
        ).start()
        pltpu.make_async_copy(
            rcot.at[:, :, source_columns], rcot_v.at[:, place], sem_load.at[6]
        ).start()
        return carry

    def load_columns(index, carry):
        pltpu.make_async_copy(
            pkv.at[:, columns(index * HEAD_DIM, HEAD_DIM)], own_columns.at[index], sem_load.at[7]
        ).start()
        return carry

    lax.fori_loop(0, 2 * KV_HEADS, load_columns, 0)
    lax.fori_loop(0, KV_HEADS * group, load_prompt_head, 0)
    lax.fori_loop(0, group, load_response_head, 0)

    row = lax.broadcasted_iota(jnp.int32, (8, 128), 0)
    lane = lax.broadcasted_iota(jnp.int32, (8, 128), 1)
    note = jnp.zeros((8, 128), jnp.int32)
    inside = lane // 16 == lax.rem(me, 8)
    for r in range(count):
        route = routes_in[r]
        note = jnp.where((row == r) & inside, route * 16 + lane % 16, note)
        note = jnp.where((row == ROUTE_ROW) & (lane == r), route, note)
        note = jnp.where((row == REWARD_ROW) & (lane == r), rewards_in[r], note)
    notes[me] = note

    settle(own_columns, sem_load.at[7])
    pl.semaphore_wait(barrier, CTX * ring - 1)

    def send_piece(step, carry):
        head = lax.rem(c + step, KV_HEADS)
        part = lax.rem(step // KV_HEADS + my_place, 2 * blocks)
        kind = part // blocks
        block = lax.rem(part, blocks)
        there_half = lax.rem(my_half + step // (KV_HEADS * 2 * blocks), halves)
        place = place_of(blocks, kind, c, block, head, there_half)
        there = there_half * plane + place
        piece = own_columns.at[kind * KV_HEADS + head, aligned(block * size, size)]
        here = (head == c) & (there == me)

        @pl.when(here)
        def _():
            pltpu.make_async_copy(piece, pieces_in.at[me], sem_piece.at[2]).start()

        @pl.when(jnp.logical_not(here))
        def _():
            remote(
                piece, pieces_in.at[me], sem_piece.at[0], sem_piece.at[1], (head, there)
            ).start()

        @pl.when(step > 0)
        def _():
            note_there = (c, moved(step))
            remote(notes.at[me], notes.at[me], sem_note.at[0], sem_note.at[1], note_there).start()

        return carry

    piece_count = halves * KV_HEADS * 2 * blocks
    lax.fori_loop(0, piece_count, send_piece, 0)

    def tile(index):
        return tiles.at[pl.ds(index * rows, rows)]

    def send_tile(src, index, slot, where):
        return remote(src, tile(index), sem_tile_send.at[slot], sem_tile_recv.at[index], (where, me))

    @pl.when(c == 0)
    def _():
        send_tile(pkv, 0, 0, 2).start()
        send_tile(pkv, 0, 1, 1).start()

    @pl.when(c == 1)
    def _():
        send_tile(pkv, 1, 0, 3).start()

    @pl.when(c == 2)
    def _():
        send_tile(pkv, 2, 0, 3).start()

    for index in range(1, CTX):

        @pl.when(c < index)
        def _():
            tiles[index * rows : (index + 1) * rows, :] = jnp.zeros((rows, 2 * half), jnp.bfloat16)

    stack = min(4, group)
    key = lax.broadcasted_iota(jnp.int32, (length, rows), 0)
    query = lax.broadcasted_iota(jnp.int32, (length, rows), 1) + c * rows
    allowed_here = jnp.where(key <= query, 0.0, -jnp.inf)
    for index in range(stack):
        bias[:, index * rows : (index + 1) * rows] = allowed_here
    self_acc[...] = jnp.zeros_like(self_acc)
    share_acc[...] = jnp.zeros_like(share_acc)

    settle(notes.at[pl.ds(0, ring - 1)], sem_note.at[1])
    every = notes[...]
    note_row = lax.broadcasted_iota(jnp.int32, every.shape, 1)
    routes = jnp.sum(jnp.where(note_row == ROUTE_ROW, every, 0), axis=1)
    rewards = jnp.sum(jnp.where(note_row == REWARD_ROW, every, 0), axis=1).astype(jnp.float32)
    picks_v[...] = routes
    to_scalars = pltpu.make_async_copy(picks_v, picks, sem_note.at[2])
    to_scalars.start()
    to_scalars.wait()

    @pl.when(c == source)
    def _():
        settle(pieces_in.at[me], sem_piece.at[2])
        settle(pieces_in.at[pl.ds(0, ring - 1)], sem_piece.at[1])

    @pl.when(c != source)
    def _():
        settle(pieces_in, sem_piece.at[1])

    def send_pick(step, carry):
        r = step // (plane - 1)
        there = moved(lax.rem(step, plane - 1) + 1)
        there_place = lax.rem(there, plane)
        picked[r, there_place] = pieces_in[picks[there, r]]
        remote(
            picked.at[r, there_place],
            chosen.at[r, aligned(my_position * size, size)],
            sem_pick_send.at[r],
            sem_pick_recv.at[r],
            (c, there),
        ).start()
        return carry

    lax.fori_loop(0, count * (plane - 1), send_pick, 0)
    for r in range(count):
        chosen[r, aligned(my_position * size, size), :] = pieces_in[picks[me, r]]

    @pl.when(c == 2)
    def _():
        settle(tile(0), sem_tile_recv.at[0])
        send_tile(tile(0), 0, 1, 3).start()
        settle(tile(1), sem_tile_recv.at[1])

    @pl.when(c == 3)
    def _():
        settle(tile(1), sem_tile_recv.at[1])
        send_tile(tile(1), 1, 0, 2).start()
        settle(tile(0), sem_tile_recv.at[0])
        settle(tile(2), sem_tile_recv.at[2])

    @pl.when(c == 1)
    def _():
        settle(tile(0), sem_tile_recv.at[0])

    own_tile.wait()
    own_tree_k.wait()
    own_tree_v.wait()
    settle(pq_v, sem_load.at[3])
    settle(pcot_v, sem_load.at[4])
    settle(rq_v, sem_load.at[5])
    settle(rcot_v, sem_load.at[6])

    parts = group // stack
    together = stack * rows

    def prompt_step(step, carry):
        head = step // parts
        key_columns = columns(head * HEAD_DIM, HEAD_DIM)
        value_columns = columns(half + head * HEAD_DIM, HEAD_DIM)
        place = aligned(step * together, together)
        grad_query, ((grad_keys, grad_values),) = attention_grads(
            pq_v[place, :],
            pcot_v[place, :],
            [(tiles[:, key_columns], tiles[:, value_columns], lambda part: part + bias[...])],
            scale,
        )
        self_acc[:, key_columns] += grad_keys * scale
        self_acc[:, value_columns] += grad_values
        turned = jnp.transpose((grad_query * scale).astype(jnp.bfloat16))
        for index in range(stack):
            dpq[:, columns((step * stack + index) * HEAD_DIM, HEAD_DIM)] = turned[
                index * rows : (index + 1) * rows
            ]
        return carry

    part_width = half // PARTS

    def self_tile(index, part):
        here = slice(index * rows, (index + 1) * rows)
        keys = slice(part * part_width, (part + 1) * part_width)
        values = slice(half + part * part_width, half + (part + 1) * part_width)
        return jnp.concatenate([self_acc[here, keys], self_acc[here, values]], axis=1)

    def send_self(values, part, slot, there, there_slot):
        self_out[part, slot] = values.astype(jnp.bfloat16)
        remote(
            self_out.at[part, slot],
            self_in.at[part, there_slot],
            sem_self_send.at[part, slot],
            sem_self_recv.at[part, there_slot],
            (there, me),
        ).start()

    def prompt_part(part):
        steps = KV_HEADS * parts // PARTS
        lax.fori_loop(part * steps, (part + 1) * steps, prompt_step, 0)

        @pl.when(c == 1)
        def _():
            send_self(self_tile(0, part), part, 0, 0, 0)

        @pl.when(c == 2)
        def _():
            send_self(self_tile(1, part), part, 0, 3, 0)

        @pl.when(c == 3)
        def _():
            send_self(self_tile(0, part), part, 0, 2, 0)
            send_self(self_tile(2, part), part, 1, 2, 1)

    def cross_self(part):
        for core, index in ((2, 0), (3, 1)):

            @pl.when(c == core)
            def _():
                settle(self_in.at[part, 0], sem_self_recv.at[part, 0])
                theirs = self_in[part, 0].astype(jnp.float32)
                send_self(self_tile(index, part) + theirs, part, 2, index, 2)

    prompt_part(0)

    note_lane = lax.broadcasted_iota(jnp.int32, routes.shape, 1)
    for r in range(count):
        same = ((routes == routes_in[r]) & (note_lane < count)).astype(jnp.float32)

        def summed(values):
            return jnp.sum(jnp.sum(values, axis=1, keepdims=True), axis=0, keepdims=True)

        number = summed(same)
        reward_sum = summed(same * rewards)
        reward_square = summed(same * rewards * rewards)
        variance = reward_square * number - reward_sum * reward_sum
        spread = jnp.sqrt(jnp.maximum(variance, number * number)) / number
        own_reward = jnp.full((1, 1), rewards_in[r], jnp.int32).astype(jnp.float32)
        advantage = (own_reward - reward_sum / number) / spread
        rcot_v[r] = (advantage * rcot_v[r].astype(jnp.float32)).astype(jnp.bfloat16)

    key_place = lax.broadcasted_iota(jnp.int32, (tokens, group * tokens), 0)
    query_place = lax.broadcasted_iota(jnp.int32, (tokens, group * tokens), 1) % tokens
    square_row = lax.broadcasted_iota(jnp.int32, (tokens, tokens), 0)
    square_column = lax.broadcasted_iota(jnp.int32, (tokens, tokens), 1)

    def query_rows(r, owner):
        return drq.at[r, :, columns(owner * width, width)]

    def response_step(r, carry):
        settle(chosen.at[r, pl.ds(0, (plane - 1) * size)], sem_pick_recv.at[r])
        ends = tree_in[pl.ds(r, 1), :]
        ends = jnp.sum(
            jnp.where(square_row == square_column, ends, 0), axis=1, keepdims=True
        )
        allowed = (key_place <= query_place) & (query_place < ends)
        grad_query, (prompt_terms, tree_terms) = attention_grads(
            rq_v[r],
            rcot_v[r],
            [
                (chosen[r, :length, :], chosen[r, length:, :], None),
                (tree_k[r], tree_v[r], lambda part: jnp.where(allowed, part, -jnp.inf)),
            ],
            scale,
        )
        grads[r, :length, :] = (prompt_terms[0] * scale).astype(jnp.bfloat16)
        grads[r, length:, :] = prompt_terms[1].astype(jnp.bfloat16)
        drkv[r, :, columns(c * HEAD_DIM, HEAD_DIM)] = (tree_terms[0] * scale).astype(jnp.bfloat16)
        drkv[r, :, columns(half + c * HEAD_DIM, HEAD_DIM)] = tree_terms[1].astype(jnp.bfloat16)
        turned = jnp.transpose((grad_query * scale).astype(jnp.bfloat16))
        drq[r, :, columns(c * width, width)] = jnp.concatenate(
            [turned[g * tokens : (g + 1) * tokens] for g in range(group)], axis=1
        )

        def send_share(step, inner):
            there = moved(step)
            remote(
                grads.at[r, aligned(position(lax.rem(there, plane)) * size, size)],
                shares.at[r, my_place],
                sem_share_send.at[r],
                sem_share_recv.at[r],
                (c, there),
            ).start()
            return inner

        mine = query_rows(r, c)
        remote(mine, mine, sem_query.at[0, r], sem_query.at[1, r], (across, me)).start()
        lax.fori_loop(1, plane, send_share, 0)
        remote(mine, mine, sem_query.at[2, r], sem_query.at[3, r], (beside, me)).start()
        shares[r, my_place] = grads[r, aligned(my_position * size, size), :]
        return carry

    lax.fori_loop(0, count, response_step, 0)

    def tree_part(kind, owner):
        return drkv.at[:, :, columns(kind * half + owner * HEAD_DIM, HEAD_DIM)]

    for kind in range(2):
        mine = tree_part(kind, c)
        remote(mine, mine, sem_tree.at[0, kind], sem_tree.at[1, kind], (across, me)).start()
        remote(mine, mine, sem_tree.at[2, kind], sem_tree.at[3, kind], (beside, me)).start()

    cross_self(0)
    for part in range(1, PARTS):
        prompt_part(part)

    subs = size // 16
    groups = plane // 8

    def share_step(r, carry):
        target = lax.broadcasted_iota(jnp.int32, (ring * 16, 128), 0)
        place = lax.broadcasted_iota(jnp.int32, (8, 8, 128), 1)
        spread = []
        for index in range(groups):
            near = notes[pl.ds(my_half * plane + index * 8, 8)]
            codes = jnp.sum(jnp.where(place == r, near, 0), axis=0)
            codes = jnp.sum(codes, axis=0, keepdims=True)
            spread.append((target == codes).astype(jnp.float32).astype(jnp.bfloat16))
        spread = jnp.concatenate(spread, axis=1)
        settle(shares.at[r, pl.ds(0, plane - 1)], sem_share_recv.at[r])
        for s in range(subs):
            part = shares[r, :, s * 16 : (s + 1) * 16, :].reshape(plane * 16, HEAD_DIM)
            share_acc[s] += dot_nn(spread, part)
        theirs = query_rows(r, across)
        settle(theirs, sem_query.at[1, r])
        remote(theirs, theirs, sem_query.at[4, r], sem_query.at[5, r], (beside, me)).start()
        return carry

    def share_steps(first, last):
        lax.fori_loop(first, last, share_step, 0)

    for part in range(1, PARTS):
        cross_self(part)
    share_steps(0, count)
    for s in range(subs):
        totals[:, s * 16 : (s + 1) * 16, :] = (
            share_acc[s].reshape(ring, 16, HEAD_DIM).astype(jnp.bfloat16)
        )

    home = returned.at[my_half, own_kind * KV_HEADS + c, aligned(own_block * size, size)]

    @pl.when(c == source)
    def _():
        pltpu.make_async_copy(totals.at[me], home, sem_total.at[2]).start()

    @pl.when(c != source)
    def _():
        remote(totals.at[me], home, sem_total.at[0], sem_total.at[1], (source, me)).start()

    def send_total(step, carry):
        there = moved(step)
        remote(
            totals.at[there], home, sem_total.at[0], sem_total.at[1], (source, there)
        ).start()
        return carry

    lax.fori_loop(1, ring, send_total, 0)

    for kind in range(2):
        theirs = tree_part(kind, across)
        settle(theirs, sem_tree.at[1, kind])
        remote(theirs, theirs, sem_tree.at[4, kind], sem_tree.at[5, kind], (beside, me)).start()

    def add_self(part, slot):
        settle(self_in.at[part, slot], sem_self_recv.at[part, slot])
        return self_in[part, slot].astype(jnp.float32)

    own_rows = pl.ds(pl.multiple_of(c * rows, rows), rows)
    for part in range(PARTS):
        keys = slice(part * part_width, (part + 1) * part_width)
        values = slice(half + part * part_width, half + (part + 1) * part_width)

        def add(more):
            self_acc[own_rows, keys] += more[:, :part_width]
            self_acc[own_rows, values] += more[:, part_width:]

        @pl.when(c == 0)
        def _():
            add(add_self(part, 0) + add_self(part, 2))

        @pl.when(c == 1)
        def _():
            add(add_self(part, 2))

        @pl.when(c == 2)
        def _():
            add(add_self(part, 1))

        @pl.when(c >= 1)
        def _():
            settle(self_out.at[part, 0], sem_self_send.at[part, 0])

        @pl.when(c == 3)
        def _():
            settle(self_out.at[part, 1], sem_self_send.at[part, 1])

        @pl.when(c >= 2)
        def _():
            settle(self_out.at[part, 2], sem_self_send.at[part, 2])

    settle(notes.at[pl.ds(0, ring - 1)], sem_note.at[0])

    @pl.when(c == source)
    def _():
        settle(pieces_in.at[pl.ds(0, piece_count - 1)], sem_piece.at[0])

    @pl.when(c != source)
    def _():
        settle(pieces_in.at[pl.ds(0, piece_count)], sem_piece.at[0])

    @pl.when(c == 0)
    def _():
        send_tile(pkv, 0, 0, 2).wait_send()
        send_tile(pkv, 0, 1, 1).wait_send()

    @pl.when(c == 1)
    def _():
        send_tile(pkv, 1, 0, 3).wait_send()

    @pl.when(c == 2)
    def _():
        send_tile(pkv, 2, 0, 3).wait_send()
        send_tile(tile(0), 0, 1, 3).wait_send()

    @pl.when(c == 3)
    def _():
        send_tile(tile(1), 1, 0, 2).wait_send()

    for r in range(count):
        settle(picked.at[r, pl.ds(0, plane - 1)], sem_pick_send.at[r])
        settle(shares.at[r, pl.ds(0, plane - 1)], sem_share_send.at[r])
        for slot in (0, 2, 3, 4, 5):
            settle(query_rows(r, c), sem_query.at[slot, r])
    for kind in range(2):
        for slot in (0, 2, 3, 4, 5):
            settle(tree_part(kind, c), sem_tree.at[slot, kind])

    @pl.when(c == source)
    def _():
        settle(totals.at[me], sem_total.at[2])
        settle(totals.at[pl.ds(0, ring - 1)], sem_total.at[0])

    @pl.when(c != source)
    def _():
        settle(totals, sem_total.at[0])

    others = halves * KV_HEADS * 2 * blocks

    @pl.when(c == source)
    def _():
        settle(totals.at[pl.ds(0, others - 1)], sem_total.at[1])

    @pl.when(c != source)
    def _():
        settle(totals.at[pl.ds(0, others)], sem_total.at[1])

    for index in range(2 * KV_HEADS):
        here = slice(index * HEAD_DIM, (index + 1) * HEAD_DIM)
        total = self_acc[own_rows, here]
        for z in range(halves):
            total = total + returned[z, index].astype(jnp.float32)
        dpkv[:, here] = total.astype(jnp.bfloat16)


def store(count, *refs):
    sources, targets, sems = refs[:count], refs[count : 2 * count], refs[2 * count]
    copies = [
        pltpu.make_async_copy(source, target, sems.at[index])
        for index, (source, target) in enumerate(zip(sources, targets))
    ]
    for copy in copies:
        copy.start()
    for copy in copies:
        copy.wait()


def body(
    prompt_q, prompt_kv, prompt_cot, resp_q, resp_kv, resp_cot, resp_prompt, tree_end, rewards
):
    ring = lax.axis_size("resp")
    rows, wide = prompt_q.shape[1:]
    kv_wide = prompt_kv.shape[2]
    count, tokens = resp_q.shape[:2]
    length = CTX * rows
    group = wide // (KV_HEADS * HEAD_DIM)
    width = group * HEAD_DIM
    halves, plane = cut(ring)
    size = 2 * length // plane
    bf16, f32, i32 = jnp.bfloat16, jnp.float32, jnp.int32
    any_space = pl.BlockSpec(memory_space=pl.ANY)
    scalars = pl.BlockSpec(memory_space=pltpu.SMEM)
    vector = pl.BlockSpec(memory_space=pltpu.VMEM)
    dma = pltpu.SemaphoreType.DMA
    dpq, dpkv, drq, drkv = pl.pallas_call(
        functools.partial(kernel, ring),
        out_shape=(
            pltpu.VMEM((rows, wide), bf16),
            pltpu.VMEM((rows, kv_wide), bf16),
            pltpu.VMEM(resp_q.shape, bf16),
            pltpu.VMEM(resp_kv.shape, bf16),
        ),
        in_specs=[scalars, scalars, vector] + [any_space] * 6,
        out_specs=(vector,) * 4,
        scratch_shapes=[
            pltpu.VMEM((wide // HEAD_DIM * rows, HEAD_DIM), bf16),
            pltpu.VMEM((wide // HEAD_DIM * rows, HEAD_DIM), bf16),
            pltpu.VMEM((length, kv_wide), bf16),
            pltpu.VMEM((kv_wide // HEAD_DIM, rows, HEAD_DIM), bf16),
            pltpu.VMEM((count, group * tokens, HEAD_DIM), bf16),
            pltpu.VMEM((count, group * tokens, HEAD_DIM), bf16),
            pltpu.VMEM((count, tokens, HEAD_DIM), bf16),
            pltpu.VMEM((count, tokens, HEAD_DIM), bf16),
            pltpu.VMEM((ring, 8, 128), i32),
            pltpu.VMEM((ring, 128), i32),
            pltpu.SMEM((ring, 128), i32),
            pltpu.VMEM((ring, size, HEAD_DIM), bf16),
            pltpu.VMEM((count, plane, size, HEAD_DIM), bf16),
            pltpu.VMEM((count, 2 * length, HEAD_DIM), bf16),
            pltpu.VMEM((length, min(4, group) * rows), f32),
            pltpu.VMEM((length, kv_wide), f32),
            pltpu.VMEM((PARTS, 3, rows, kv_wide // PARTS), bf16),
            pltpu.VMEM((PARTS, 3, rows, kv_wide // PARTS), bf16),
            pltpu.VMEM((count, 2 * length, HEAD_DIM), bf16),
            pltpu.VMEM((count, plane, size, HEAD_DIM), bf16),
            pltpu.VMEM((size // 16, ring * 16, HEAD_DIM), f32),
            pltpu.VMEM((ring, size, HEAD_DIM), bf16),
            pltpu.VMEM((halves, kv_wide // HEAD_DIM, rows, HEAD_DIM), bf16),
            dma((8,)),
            dma((3,)),
            dma((3,)),
            dma((2,)),
            dma((CTX,)),
            dma((count,)),
            dma((count,)),
            dma((PARTS, 3)),
            dma((PARTS, 3)),
            dma((count,)),
            dma((count,)),
            dma((6, count)),
            dma((6, 2)),
            dma((3,)),
        ],
        compiler_params=pltpu.CompilerParams(
            collective_id=0, has_side_effects=True, vmem_limit_bytes=52 * 1024 * 1024
        ),
        name="attention_gradients",
    )(
        resp_prompt[:, 0],
        rewards,
        tree_end,
        prompt_q[0],
        prompt_kv[0],
        prompt_cot[0],
        resp_q,
        resp_kv,
        resp_cot,
    )
    results = (dpq, dpkv, drq, drkv)
    dpq, dpkv, drq, drkv = pl.pallas_call(
        functools.partial(store, len(results)),
        out_shape=[jax.ShapeDtypeStruct(result.shape, result.dtype) for result in results],
        in_specs=[vector] * len(results),
        out_specs=[any_space] * len(results),
        scratch_shapes=[dma((len(results),))],
        compiler_params=pltpu.CompilerParams(vmem_limit_bytes=16 * 1024 * 1024),
        name="store_outputs",
    )(*results)
    return (dpq[None], dpkv[None], drq, drkv)


def solution(mesh):
    in_specs = (
        P("resp", "ctx", None),
        P("resp", "ctx", None),
        P("resp", "ctx", None),
        P("resp", None, None),
        P("resp", None, None),
        P("resp", None, None),
        P("resp", None),
        P("resp", None),
        P("resp"),
    )
    out_specs = (
        P("resp", "ctx", None),
        P("resp", "ctx", None),
        P("resp", None, None),
        P("resp", None, None),
    )
    return jax.shard_map(body, mesh=mesh, in_specs=in_specs, out_specs=out_specs, check_vma=False)
```

```python
import functools
import math

import jax
import jax.numpy as jnp
from jax import lax
from jax.experimental import pallas as pl
from jax.experimental.pallas import tpu as pltpu
from jax.sharding import PartitionSpec as P

MESH = pl.DeviceIdType.MESH
KV_HEADS = 4
HEAD_DIM = 128
CTX = 4
ROUTE_ROW = 4
REWARD_ROW = 5
PARTS = 2


def dot_nt(a, b):
    return lax.dot_general(a, b, (((1,), (1,)), ((), ())), preferred_element_type=jnp.float32)


def dot_tn(a, b):
    return lax.dot_general(a, b, (((0,), (0,)), ((), ())), preferred_element_type=jnp.float32)


def dot_nn(a, b):
    return lax.dot_general(a, b, (((1,), (0,)), ((), ())), preferred_element_type=jnp.float32)


def aligned(start, size):
    return pl.ds(pl.multiple_of(start, 16), size)


def columns(start, size):
    return pl.ds(pl.multiple_of(start, 128), size)


def attention_grads(queries, cotangent, pieces, scale):
    to_power = scale * math.log2(math.e)
    scores = []
    for keys, values, adjust in pieces:
        part = dot_nt(keys, queries) * to_power
        scores.append(part if adjust is None else adjust(part))
    highest = functools.reduce(
        jnp.maximum, [jnp.max(part, axis=0, keepdims=True) for part in scores]
    )
    powers = [jnp.exp2(part - highest) for part in scores]
    total = functools.reduce(jnp.add, [jnp.sum(part, axis=0, keepdims=True) for part in powers])
    inverse = 1.0 / total
    grad_probs = [dot_nt(values, cotangent) for keys, values, adjust in pieces]
    delta = inverse * functools.reduce(
        jnp.add,
        [jnp.sum(a * b, axis=0, keepdims=True) for a, b in zip(powers, grad_probs)],
    )
    grad_query = None
    grads = []
    for (keys, values, adjust), power, grad_prob in zip(pieces, powers, grad_probs):
        weight = power * inverse
        narrow = weight.astype(jnp.bfloat16)
        grad_score = (weight * (grad_prob - delta)).astype(jnp.bfloat16)
        grad_values = dot_nn(narrow, cotangent)
        grad_keys = dot_nn(grad_score, queries)
        term = dot_tn(keys, grad_score)
        grad_query = term if grad_query is None else grad_query + term
        grads.append((grad_keys, grad_values))
    return grad_query, grads


def cut(ring):
    halves = 2 if ring >= 16 else 1
    return halves, ring // halves


def place_of(blocks, kind, ctx, block, head, z):
    if blocks != 2:
        return (kind * CTX + ctx) * blocks + block
    high, low = head // 2, head % 2
    y_high = lax.rem(ctx % 2 + high, 2)
    y_low = lax.rem(ctx // 2 + high, 2)
    x_high = lax.rem(kind + high + low + z, 2)
    x_low = lax.rem(block + low, 2)
    return ((y_high * 2 + y_low) * 2 + x_high) * 2 + x_low


def held_at(blocks, place, head, z):
    if blocks != 2:
        return place // (CTX * blocks), lax.rem(place // blocks, CTX), lax.rem(place, blocks)
    high, low = head // 2, head % 2
    ctx = lax.rem(place // 8 + high, 2) + 2 * lax.rem(lax.rem(place // 4, 2) + high, 2)
    kind = lax.rem(lax.rem(place // 2, 2) + high + low + z, 2)
    return kind, ctx, lax.rem(lax.rem(place, 2) + low, 2)


def kernel(
    ring,
    routes_in,
    rewards_in,
    tree_in,
    pq,
    pkv,
    pcot,
    rq,
    rkv,
    rcot,
    dpq,
    dpkv,
    drq,
    drkv,
    pq_v,
    pcot_v,
    tiles,
    own_columns,
    rq_v,
    rcot_v,
    tree_k,
    tree_v,
    notes,
    picks_v,
    picks,
    pieces_in,
    picked,
    chosen,
    bias,
    self_acc,
    self_out,
    self_in,
    grads,
    shares,
    share_acc,
    totals,
    returned,
    sem_load,
    sem_note,
    sem_piece,
    sem_tile_send,
    sem_tile_recv,
    sem_pick_send,
    sem_pick_recv,
    sem_self_send,
    sem_self_recv,
    sem_share_send,
    sem_share_recv,
    sem_query,
    sem_tree,
    sem_total,
):
    scale = 1.0 / math.sqrt(HEAD_DIM)
    c = lax.axis_index("ctx")
    me = lax.axis_index("resp")
    rows = pq.shape[0]
    length = CTX * rows
    count, tokens = rq.shape[0], rq.shape[1]
    group = pq.shape[1] // (KV_HEADS * HEAD_DIM)
    width = group * HEAD_DIM
    half = KV_HEADS * HEAD_DIM
    halves, plane = cut(ring)
    size = 2 * length // plane
    blocks = rows // size
    my_half = me // plane
    my_place = lax.rem(me, plane)
    own_kind, source, own_block = held_at(blocks, my_place, c, my_half)

    def position(place):
        kind, ctx, block = held_at(blocks, place, c, my_half)
        return (kind * CTX + ctx) * blocks + block

    my_position = position(my_place)
    beside = c + 1 - 2 * lax.rem(c, 2)
    across = lax.rem(c + 2, CTX)
    x_size = 4
    y_size = plane // x_size

    def moved(step):
        x = lax.rem(lax.rem(me, x_size) + lax.rem(step, x_size), x_size)
        y = lax.rem(lax.rem(me // x_size, y_size) + lax.rem(step // x_size, y_size), y_size)
        z = lax.rem(my_half + step // plane, halves)
        return z * plane + y * x_size + x

    def remote(src, dst, send, recv, where):
        return pltpu.make_async_remote_copy(
            src_ref=src,
            dst_ref=dst,
            send_sem=send,
            recv_sem=recv,
            device_id=where,
            device_id_type=MESH,
        )

    def settle(ref, sem):
        pltpu.make_async_copy(ref, ref, sem).wait()

    own_tile = pltpu.make_async_copy(pkv, tiles.at[aligned(c * rows, rows)], sem_load.at[0])
    own_tree_k = pltpu.make_async_copy(
        rkv.at[:, :, columns(c * HEAD_DIM, HEAD_DIM)], tree_k, sem_load.at[1]
    )
    own_tree_v = pltpu.make_async_copy(
        rkv.at[:, :, columns(half + c * HEAD_DIM, HEAD_DIM)], tree_v, sem_load.at[2]
    )

    barrier = pltpu.get_barrier_semaphore()

    def greet(step, carry):
        there = (lax.rem(c + step // ring, CTX), lax.rem(me + lax.rem(step, ring), ring))
        pl.semaphore_signal(barrier, inc=1, device_id=there, device_id_type=MESH)
        return carry

    lax.fori_loop(1, CTX * ring, greet, 0)

    own_tile.start()
    own_tree_k.start()
    own_tree_v.start()

    def load_prompt_head(head, carry):
        source_columns = columns(head * HEAD_DIM, HEAD_DIM)
        place = aligned(head * rows, rows)
        pltpu.make_async_copy(pq.at[:, source_columns], pq_v.at[place], sem_load.at[3]).start()
        pltpu.make_async_copy(pcot.at[:, source_columns], pcot_v.at[place], sem_load.at[4]).start()
        return carry

    def load_response_head(head, carry):
        source_columns = columns(c * width + head * HEAD_DIM, HEAD_DIM)
        place = aligned(head * tokens, tokens)
        pltpu.make_async_copy(
            rq.at[:, :, source_columns], rq_v.at[:, place], sem_load.at[5]
        ).start()
        pltpu.make_async_copy(
            rcot.at[:, :, source_columns], rcot_v.at[:, place], sem_load.at[6]
        ).start()
        return carry

    def load_columns(index, carry):
        pltpu.make_async_copy(
            pkv.at[:, columns(index * HEAD_DIM, HEAD_DIM)], own_columns.at[index], sem_load.at[7]
        ).start()
        return carry

    lax.fori_loop(0, 2 * KV_HEADS, load_columns, 0)
    lax.fori_loop(0, KV_HEADS * group, load_prompt_head, 0)
    lax.fori_loop(0, group, load_response_head, 0)

    row = lax.broadcasted_iota(jnp.int32, (8, 128), 0)
    lane = lax.broadcasted_iota(jnp.int32, (8, 128), 1)
    note = jnp.zeros((8, 128), jnp.int32)
    inside = lane // 16 == lax.rem(me, 8)
    for r in range(count):
        route = routes_in[r]
        note = jnp.where((row == r) & inside, route * 16 + lane % 16, note)
        note = jnp.where((row == ROUTE_ROW) & (lane == r), route, note)
        note = jnp.where((row == REWARD_ROW) & (lane == r), rewards_in[r], note)
    notes[me] = note

    settle(own_columns, sem_load.at[7])
    pl.semaphore_wait(barrier, CTX * ring - 1)

    piece_count = halves * KV_HEADS * 2 * blocks

    def send_piece(step, carry):
        index = lax.rem(step + me, piece_count)
        head = lax.rem(index // (2 * blocks), KV_HEADS)
        kind = lax.rem(index, 2 * blocks) // blocks
        block = lax.rem(index, blocks)
        there_half = index // (KV_HEADS * 2 * blocks)
        place = place_of(blocks, kind, c, block, head, there_half)
        there = there_half * plane + place
        piece = own_columns.at[kind * KV_HEADS + head, aligned(block * size, size)]
        here = (head == c) & (there == me)

        @pl.when(here)
        def _():
            pltpu.make_async_copy(piece, pieces_in.at[me], sem_piece.at[2]).start()

        @pl.when(jnp.logical_not(here))
        def _():
            remote(
                piece, pieces_in.at[me], sem_piece.at[0], sem_piece.at[1], (head, there)
            ).start()

        @pl.when(step > 0)
        def _():
            note_there = (c, moved(step))
            remote(notes.at[me], notes.at[me], sem_note.at[0], sem_note.at[1], note_there).start()

        return carry

    lax.fori_loop(0, piece_count, send_piece, 0)

    def tile(index):
        return tiles.at[pl.ds(index * rows, rows)]

    def send_tile(src, index, slot, where):
        return remote(src, tile(index), sem_tile_send.at[slot], sem_tile_recv.at[index], (where, me))

    @pl.when(c == 0)
    def _():
        send_tile(pkv, 0, 0, 2).start()
        send_tile(pkv, 0, 1, 1).start()

    @pl.when(c == 1)
    def _():
        send_tile(pkv, 1, 0, 3).start()

    @pl.when(c == 2)
    def _():
        send_tile(pkv, 2, 0, 3).start()

    for index in range(1, CTX):

        @pl.when(c < index)
        def _():
            tiles[index * rows : (index + 1) * rows, :] = jnp.zeros((rows, 2 * half), jnp.bfloat16)

    stack = min(8, group)
    key = lax.broadcasted_iota(jnp.int32, (length, rows), 0)
    query = lax.broadcasted_iota(jnp.int32, (length, rows), 1) + c * rows
    allowed_here = jnp.where(key <= query, 0.0, -jnp.inf)
    for index in range(stack):
        bias[:, index * rows : (index + 1) * rows] = allowed_here
    self_acc[...] = jnp.zeros_like(self_acc)
    share_acc[...] = jnp.zeros_like(share_acc)

    settle(notes.at[pl.ds(0, ring - 1)], sem_note.at[1])
    every = notes[...]
    note_row = lax.broadcasted_iota(jnp.int32, every.shape, 1)
    routes = jnp.sum(jnp.where(note_row == ROUTE_ROW, every, 0), axis=1)
    rewards = jnp.sum(jnp.where(note_row == REWARD_ROW, every, 0), axis=1).astype(jnp.float32)
    picks_v[...] = routes
    to_scalars = pltpu.make_async_copy(picks_v, picks, sem_note.at[2])
    to_scalars.start()
    to_scalars.wait()

    @pl.when(c == source)
    def _():
        settle(pieces_in.at[me], sem_piece.at[2])
        settle(pieces_in.at[pl.ds(0, ring - 1)], sem_piece.at[1])

    @pl.when(c != source)
    def _():
        settle(pieces_in, sem_piece.at[1])

    def send_pick(step, carry):
        r = step // (plane - 1)
        there = moved(lax.rem(step, plane - 1) + 1)
        there_place = lax.rem(there, plane)
        picked[r, there_place] = pieces_in[picks[there, r]]
        remote(
            picked.at[r, there_place],
            chosen.at[r, aligned(my_position * size, size)],
            sem_pick_send.at[r],
            sem_pick_recv.at[r],
            (c, there),
        ).start()
        return carry

    lax.fori_loop(0, count * (plane - 1), send_pick, 0)
    for r in range(count):
        chosen[r, aligned(my_position * size, size), :] = pieces_in[picks[me, r]]

    @pl.when(c == 2)
    def _():
        settle(tile(0), sem_tile_recv.at[0])
        send_tile(tile(0), 0, 1, 3).start()
        settle(tile(1), sem_tile_recv.at[1])

    @pl.when(c == 3)
    def _():
        settle(tile(1), sem_tile_recv.at[1])
        send_tile(tile(1), 1, 0, 2).start()
        settle(tile(0), sem_tile_recv.at[0])
        settle(tile(2), sem_tile_recv.at[2])

    @pl.when(c == 1)
    def _():
        settle(tile(0), sem_tile_recv.at[0])

    own_tile.wait()
    own_tree_k.wait()
    own_tree_v.wait()
    settle(pq_v, sem_load.at[3])
    settle(pcot_v, sem_load.at[4])
    settle(rq_v, sem_load.at[5])
    settle(rcot_v, sem_load.at[6])

    parts = group // stack
    together = stack * rows

    def prompt_step(step, carry):
        head = step // parts
        key_columns = columns(head * HEAD_DIM, HEAD_DIM)
        value_columns = columns(half + head * HEAD_DIM, HEAD_DIM)
        place = aligned(step * together, together)
        grad_query, ((grad_keys, grad_values),) = attention_grads(
            pq_v[place, :],
            pcot_v[place, :],
            [(tiles[:, key_columns], tiles[:, value_columns], lambda part: part + bias[...])],
            scale,
        )
        self_acc[:, key_columns] += grad_keys * scale
        self_acc[:, value_columns] += grad_values
        turned = jnp.transpose((grad_query * scale).astype(jnp.bfloat16))
        for index in range(stack):
            dpq[:, columns((step * stack + index) * HEAD_DIM, HEAD_DIM)] = turned[
                index * rows : (index + 1) * rows
            ]
        return carry

    part_width = half // PARTS

    def self_tile(index, part):
        here = slice(index * rows, (index + 1) * rows)
        keys = slice(part * part_width, (part + 1) * part_width)
        values = slice(half + part * part_width, half + (part + 1) * part_width)
        return jnp.concatenate([self_acc[here, keys], self_acc[here, values]], axis=1)

    def send_self(values, part, slot, there, there_slot):
        self_out[part, slot] = values.astype(jnp.bfloat16)
        remote(
            self_out.at[part, slot],
            self_in.at[part, there_slot],
            sem_self_send.at[part, slot],
            sem_self_recv.at[part, there_slot],
            (there, me),
        ).start()

    def prompt_part(part):
        steps = KV_HEADS * parts // PARTS
        lax.fori_loop(part * steps, (part + 1) * steps, prompt_step, 0)

        @pl.when(c == 1)
        def _():
            send_self(self_tile(0, part), part, 0, 0, 0)

        @pl.when(c == 2)
        def _():
            send_self(self_tile(1, part), part, 0, 3, 0)

        @pl.when(c == 3)
        def _():
            send_self(self_tile(0, part), part, 0, 2, 0)
            send_self(self_tile(2, part), part, 1, 2, 1)

    def cross_self(part):
        for core, index in ((2, 0), (3, 1)):

            @pl.when(c == core)
            def _():
                settle(self_in.at[part, 0], sem_self_recv.at[part, 0])
                theirs = self_in[part, 0].astype(jnp.float32)
                send_self(self_tile(index, part) + theirs, part, 2, index, 2)

    prompt_part(0)

    note_lane = lax.broadcasted_iota(jnp.int32, routes.shape, 1)
    for r in range(count):
        same = ((routes == routes_in[r]) & (note_lane < count)).astype(jnp.float32)

        def summed(values):
            return jnp.sum(jnp.sum(values, axis=1, keepdims=True), axis=0, keepdims=True)

        number = summed(same)
        reward_sum = summed(same * rewards)
        reward_square = summed(same * rewards * rewards)
        variance = reward_square * number - reward_sum * reward_sum
        spread = jnp.sqrt(jnp.maximum(variance, number * number)) / number
        own_reward = jnp.full((1, 1), rewards_in[r], jnp.int32).astype(jnp.float32)
        advantage = (own_reward - reward_sum / number) / spread
        rcot_v[r] = (advantage * rcot_v[r].astype(jnp.float32)).astype(jnp.bfloat16)

    key_place = lax.broadcasted_iota(jnp.int32, (tokens, group * tokens), 0)
    query_place = lax.broadcasted_iota(jnp.int32, (tokens, group * tokens), 1) % tokens
    square_row = lax.broadcasted_iota(jnp.int32, (tokens, tokens), 0)
    square_column = lax.broadcasted_iota(jnp.int32, (tokens, tokens), 1)

    def query_rows(r, owner):
        return drq.at[r, :, columns(owner * width, width)]

    def response_step(r, carry):
        settle(chosen.at[r, pl.ds(0, (plane - 1) * size)], sem_pick_recv.at[r])
        ends = tree_in[pl.ds(r, 1), :]
        ends = jnp.sum(
            jnp.where(square_row == square_column, ends, 0), axis=1, keepdims=True
        )
        allowed = (key_place <= query_place) & (query_place < ends)
        grad_query, (prompt_terms, tree_terms) = attention_grads(
            rq_v[r],
            rcot_v[r],
            [
                (chosen[r, :length, :], chosen[r, length:, :], None),
                (tree_k[r], tree_v[r], lambda part: jnp.where(allowed, part, -jnp.inf)),
            ],
            scale,
        )
        grads[r, :length, :] = (prompt_terms[0] * scale).astype(jnp.bfloat16)
        grads[r, length:, :] = prompt_terms[1].astype(jnp.bfloat16)
        drkv[r, :, columns(c * HEAD_DIM, HEAD_DIM)] = (tree_terms[0] * scale).astype(jnp.bfloat16)
        drkv[r, :, columns(half + c * HEAD_DIM, HEAD_DIM)] = tree_terms[1].astype(jnp.bfloat16)
        turned = jnp.transpose((grad_query * scale).astype(jnp.bfloat16))
        drq[r, :, columns(c * width, width)] = jnp.concatenate(
            [turned[g * tokens : (g + 1) * tokens] for g in range(group)], axis=1
        )

        def send_share(step, inner):
            there = moved(step)
            remote(
                grads.at[r, aligned(position(lax.rem(there, plane)) * size, size)],
                shares.at[r, my_place],
                sem_share_send.at[r],
                sem_share_recv.at[r],
                (c, there),
            ).start()
            return inner

        mine = query_rows(r, c)
        remote(mine, mine, sem_query.at[0, r], sem_query.at[1, r], (across, me)).start()
        lax.fori_loop(1, plane, send_share, 0)
        remote(mine, mine, sem_query.at[2, r], sem_query.at[3, r], (beside, me)).start()
        shares[r, my_place] = grads[r, aligned(my_position * size, size), :]
        return carry

    lax.fori_loop(0, count, response_step, 0)

    def tree_part(kind, owner):
        return drkv.at[:, :, columns(kind * half + owner * HEAD_DIM, HEAD_DIM)]

    for kind in range(2):
        mine = tree_part(kind, c)
        remote(mine, mine, sem_tree.at[0, kind], sem_tree.at[1, kind], (across, me)).start()
        remote(mine, mine, sem_tree.at[2, kind], sem_tree.at[3, kind], (beside, me)).start()

    cross_self(0)
    for part in range(1, PARTS):
        prompt_part(part)

    subs = size // 16
    groups = plane // 8

    def share_step(r, carry):
        target = lax.broadcasted_iota(jnp.int32, (ring * 16, 128), 0)
        place = lax.broadcasted_iota(jnp.int32, (8, 8, 128), 1)
        spread = []
        for index in range(groups):
            near = notes[pl.ds(my_half * plane + index * 8, 8)]
            codes = jnp.sum(jnp.where(place == r, near, 0), axis=0)
            codes = jnp.sum(codes, axis=0, keepdims=True)
            spread.append((target == codes).astype(jnp.float32).astype(jnp.bfloat16))
        spread = jnp.concatenate(spread, axis=1)
        settle(shares.at[r, pl.ds(0, plane - 1)], sem_share_recv.at[r])
        for s in range(subs):
            part = shares[r, :, s * 16 : (s + 1) * 16, :].reshape(plane * 16, HEAD_DIM)
            share_acc[s] += dot_nn(spread, part)
        theirs = query_rows(r, across)
        settle(theirs, sem_query.at[1, r])
        remote(theirs, theirs, sem_query.at[4, r], sem_query.at[5, r], (beside, me)).start()
        return carry

    def share_steps(first, last):
        lax.fori_loop(first, last, share_step, 0)

    for part in range(1, PARTS):
        cross_self(part)
    share_steps(0, count)
    for s in range(subs):
        totals[:, s * 16 : (s + 1) * 16, :] = (
            share_acc[s].reshape(ring, 16, HEAD_DIM).astype(jnp.bfloat16)
        )

    home = returned.at[my_half, own_kind * KV_HEADS + c, aligned(own_block * size, size)]

    @pl.when(c == source)
    def _():
        pltpu.make_async_copy(totals.at[me], home, sem_total.at[2]).start()

    @pl.when(c != source)
    def _():
        remote(totals.at[me], home, sem_total.at[0], sem_total.at[1], (source, me)).start()

    def send_total(step, carry):
        there = moved(step)
        remote(
            totals.at[there], home, sem_total.at[0], sem_total.at[1], (source, there)
        ).start()
        return carry

    lax.fori_loop(1, ring, send_total, 0)

    for kind in range(2):
        theirs = tree_part(kind, across)
        settle(theirs, sem_tree.at[1, kind])
        remote(theirs, theirs, sem_tree.at[4, kind], sem_tree.at[5, kind], (beside, me)).start()

    def add_self(part, slot):
        settle(self_in.at[part, slot], sem_self_recv.at[part, slot])
        return self_in[part, slot].astype(jnp.float32)

    own_rows = pl.ds(pl.multiple_of(c * rows, rows), rows)
    for part in range(PARTS):
        keys = slice(part * part_width, (part + 1) * part_width)
        values = slice(half + part * part_width, half + (part + 1) * part_width)

        def add(more):
            self_acc[own_rows, keys] += more[:, :part_width]
            self_acc[own_rows, values] += more[:, part_width:]

        @pl.when(c == 0)
        def _():
            add(add_self(part, 0) + add_self(part, 2))

        @pl.when(c == 1)
        def _():
            add(add_self(part, 2))

        @pl.when(c == 2)
        def _():
            add(add_self(part, 1))

        @pl.when(c >= 1)
        def _():
            settle(self_out.at[part, 0], sem_self_send.at[part, 0])

        @pl.when(c == 3)
        def _():
            settle(self_out.at[part, 1], sem_self_send.at[part, 1])

        @pl.when(c >= 2)
        def _():
            settle(self_out.at[part, 2], sem_self_send.at[part, 2])

    settle(notes.at[pl.ds(0, ring - 1)], sem_note.at[0])

    @pl.when(c == source)
    def _():
        settle(pieces_in.at[pl.ds(0, piece_count - 1)], sem_piece.at[0])

    @pl.when(c != source)
    def _():
        settle(pieces_in.at[pl.ds(0, piece_count)], sem_piece.at[0])

    @pl.when(c == 0)
    def _():
        send_tile(pkv, 0, 0, 2).wait_send()
        send_tile(pkv, 0, 1, 1).wait_send()

    @pl.when(c == 1)
    def _():
        send_tile(pkv, 1, 0, 3).wait_send()

    @pl.when(c == 2)
    def _():
        send_tile(pkv, 2, 0, 3).wait_send()
        send_tile(tile(0), 0, 1, 3).wait_send()

    @pl.when(c == 3)
    def _():
        send_tile(tile(1), 1, 0, 2).wait_send()

    for r in range(count):
        settle(picked.at[r, pl.ds(0, plane - 1)], sem_pick_send.at[r])
        settle(shares.at[r, pl.ds(0, plane - 1)], sem_share_send.at[r])
        for slot in (0, 2, 3, 4, 5):
            settle(query_rows(r, c), sem_query.at[slot, r])
    for kind in range(2):
        for slot in (0, 2, 3, 4, 5):
            settle(tree_part(kind, c), sem_tree.at[slot, kind])

    @pl.when(c == source)
    def _():
        settle(totals.at[me], sem_total.at[2])
        settle(totals.at[pl.ds(0, ring - 1)], sem_total.at[0])

    @pl.when(c != source)
    def _():
        settle(totals, sem_total.at[0])

    others = halves * KV_HEADS * 2 * blocks

    @pl.when(c == source)
    def _():
        settle(totals.at[pl.ds(0, others - 1)], sem_total.at[1])

    @pl.when(c != source)
    def _():
        settle(totals.at[pl.ds(0, others)], sem_total.at[1])

    for index in range(2 * KV_HEADS):
        here = slice(index * HEAD_DIM, (index + 1) * HEAD_DIM)
        total = self_acc[own_rows, here]
        for z in range(halves):
            total = total + returned[z, index].astype(jnp.float32)
        dpkv[:, here] = total.astype(jnp.bfloat16)


def store(count, *refs):
    sources, targets, sems = refs[:count], refs[count : 2 * count], refs[2 * count]
    copies = [
        pltpu.make_async_copy(source, target, sems.at[index])
        for index, (source, target) in enumerate(zip(sources, targets))
    ]
    for copy in copies:
        copy.start()
    for copy in copies:
        copy.wait()


def body(
    prompt_q, prompt_kv, prompt_cot, resp_q, resp_kv, resp_cot, resp_prompt, tree_end, rewards
):
    ring = lax.axis_size("resp")
    rows, wide = prompt_q.shape[1:]
    kv_wide = prompt_kv.shape[2]
    count, tokens = resp_q.shape[:2]
    length = CTX * rows
    group = wide // (KV_HEADS * HEAD_DIM)
    width = group * HEAD_DIM
    halves, plane = cut(ring)
    size = 2 * length // plane
    bf16, f32, i32 = jnp.bfloat16, jnp.float32, jnp.int32
    any_space = pl.BlockSpec(memory_space=pl.ANY)
    scalars = pl.BlockSpec(memory_space=pltpu.SMEM)
    vector = pl.BlockSpec(memory_space=pltpu.VMEM)
    dma = pltpu.SemaphoreType.DMA
    dpq, dpkv, drq, drkv = pl.pallas_call(
        functools.partial(kernel, ring),
        out_shape=(
            pltpu.VMEM((rows, wide), bf16),
            pltpu.VMEM((rows, kv_wide), bf16),
            pltpu.VMEM(resp_q.shape, bf16),
            pltpu.VMEM(resp_kv.shape, bf16),
        ),
        in_specs=[scalars, scalars, vector] + [any_space] * 6,
        out_specs=(vector,) * 4,
        scratch_shapes=[
            pltpu.VMEM((wide // HEAD_DIM * rows, HEAD_DIM), bf16),
            pltpu.VMEM((wide // HEAD_DIM * rows, HEAD_DIM), bf16),
            pltpu.VMEM((length, kv_wide), bf16),
            pltpu.VMEM((kv_wide // HEAD_DIM, rows, HEAD_DIM), bf16),
            pltpu.VMEM((count, group * tokens, HEAD_DIM), bf16),
            pltpu.VMEM((count, group * tokens, HEAD_DIM), bf16),
            pltpu.VMEM((count, tokens, HEAD_DIM), bf16),
            pltpu.VMEM((count, tokens, HEAD_DIM), bf16),
            pltpu.VMEM((ring, 8, 128), i32),
            pltpu.VMEM((ring, 128), i32),
            pltpu.SMEM((ring, 128), i32),
            pltpu.VMEM((ring, size, HEAD_DIM), bf16),
            pltpu.VMEM((count, plane, size, HEAD_DIM), bf16),
            pltpu.VMEM((count, 2 * length, HEAD_DIM), bf16),
            pltpu.VMEM((length, min(8, group) * rows), f32),
            pltpu.VMEM((length, kv_wide), f32),
            pltpu.VMEM((PARTS, 3, rows, kv_wide // PARTS), bf16),
            pltpu.VMEM((PARTS, 3, rows, kv_wide // PARTS), bf16),
            pltpu.VMEM((count, 2 * length, HEAD_DIM), bf16),
            pltpu.VMEM((count, plane, size, HEAD_DIM), bf16),
            pltpu.VMEM((size // 16, ring * 16, HEAD_DIM), f32),
            pltpu.VMEM((ring, size, HEAD_DIM), bf16),
            pltpu.VMEM((halves, kv_wide // HEAD_DIM, rows, HEAD_DIM), bf16),
            dma((8,)),
            dma((3,)),
            dma((3,)),
            dma((2,)),
            dma((CTX,)),
            dma((count,)),
            dma((count,)),
            dma((PARTS, 3)),
            dma((PARTS, 3)),
            dma((count,)),
            dma((count,)),
            dma((6, count)),
            dma((6, 2)),
            dma((3,)),
        ],
        compiler_params=pltpu.CompilerParams(
            collective_id=0, has_side_effects=True, vmem_limit_bytes=52 * 1024 * 1024
        ),
        name="attention_gradients",
    )(
        resp_prompt[:, 0],
        rewards,
        tree_end,
        prompt_q[0],
        prompt_kv[0],
        prompt_cot[0],
        resp_q,
        resp_kv,
        resp_cot,
    )
    results = (dpq, dpkv, drq, drkv)
    dpq, dpkv, drq, drkv = pl.pallas_call(
        functools.partial(store, len(results)),
        out_shape=[jax.ShapeDtypeStruct(result.shape, result.dtype) for result in results],
        in_specs=[vector] * len(results),
        out_specs=[any_space] * len(results),
        scratch_shapes=[dma((len(results),))],
        compiler_params=pltpu.CompilerParams(vmem_limit_bytes=16 * 1024 * 1024),
        name="store_outputs",
    )(*results)
    return (dpq[None], dpkv[None], drq, drkv)


def solution(mesh):
    in_specs = (
        P("resp", "ctx", None),
        P("resp", "ctx", None),
        P("resp", "ctx", None),
        P("resp", None, None),
        P("resp", None, None),
        P("resp", None, None),
        P("resp", None),
        P("resp", None),
        P("resp"),
    )
    out_specs = (
        P("resp", "ctx", None),
        P("resp", "ctx", None),
        P("resp", None, None),
        P("resp", None, None),
    )
    return jax.shard_map(body, mesh=mesh, in_specs=in_specs, out_specs=out_specs, check_vma=False)
```

```python
import functools
import math

import jax
import jax.numpy as jnp
from jax import lax
from jax.experimental import pallas as pl
from jax.experimental.pallas import tpu as pltpu
from jax.sharding import PartitionSpec as P

MESH = pl.DeviceIdType.MESH
KV_HEADS = 4
HEAD_DIM = 128
CTX = 4
ROUTE_ROW = 4
REWARD_ROW = 5
PARTS = 2


def dot_nt(a, b):
    return lax.dot_general(a, b, (((1,), (1,)), ((), ())), preferred_element_type=jnp.float32)


def dot_tn(a, b):
    return lax.dot_general(a, b, (((0,), (0,)), ((), ())), preferred_element_type=jnp.float32)


def dot_nn(a, b):
    return lax.dot_general(a, b, (((1,), (0,)), ((), ())), preferred_element_type=jnp.float32)


def aligned(start, size):
    return pl.ds(pl.multiple_of(start, 16), size)


def columns(start, size):
    return pl.ds(pl.multiple_of(start, 128), size)


def attention_grads(queries, cotangent, pieces, scale):
    to_power = scale * math.log2(math.e)
    scores = []
    for keys, values, adjust in pieces:
        part = dot_nt(keys, queries) * to_power
        scores.append(part if adjust is None else adjust(part))
    highest = functools.reduce(
        jnp.maximum, [jnp.max(part, axis=0, keepdims=True) for part in scores]
    )
    powers = [jnp.exp2(part - highest) for part in scores]
    total = functools.reduce(jnp.add, [jnp.sum(part, axis=0, keepdims=True) for part in powers])
    inverse = 1.0 / total
    grad_probs = [dot_nt(values, cotangent) for keys, values, adjust in pieces]
    delta = inverse * functools.reduce(
        jnp.add,
        [jnp.sum(a * b, axis=0, keepdims=True) for a, b in zip(powers, grad_probs)],
    )
    grad_query = None
    grads = []
    for (keys, values, adjust), power, grad_prob in zip(pieces, powers, grad_probs):
        weight = power * inverse
        narrow = weight.astype(jnp.bfloat16)
        grad_score = (weight * (grad_prob - delta)).astype(jnp.bfloat16)
        grad_values = dot_nn(narrow, cotangent)
        grad_keys = dot_nn(grad_score, queries)
        term = dot_tn(keys, grad_score)
        grad_query = term if grad_query is None else grad_query + term
        grads.append((grad_keys, grad_values))
    return grad_query, grads


def cut(ring):
    halves = 2 if ring >= 16 else 1
    return halves, ring // halves


def place_of(blocks, kind, ctx, block, head, z):
    if blocks != 2:
        return (kind * CTX + ctx) * blocks + block
    high, low = head // 2, head % 2
    y_high = lax.rem(ctx % 2 + high, 2)
    y_low = lax.rem(ctx // 2 + high, 2)
    x_high = lax.rem(kind + high + low + z, 2)
    x_low = lax.rem(block + low, 2)
    return ((y_high * 2 + y_low) * 2 + x_high) * 2 + x_low


def held_at(blocks, place, head, z):
    if blocks != 2:
        return place // (CTX * blocks), lax.rem(place // blocks, CTX), lax.rem(place, blocks)
    high, low = head // 2, head % 2
    ctx = lax.rem(place // 8 + high, 2) + 2 * lax.rem(lax.rem(place // 4, 2) + high, 2)
    kind = lax.rem(lax.rem(place // 2, 2) + high + low + z, 2)
    return kind, ctx, lax.rem(lax.rem(place, 2) + low, 2)


def kernel(
    ring,
    routes_in,
    rewards_in,
    tree_in,
    pq,
    pkv,
    pcot,
    rq,
    rkv,
    rcot,
    dpq,
    dpkv,
    drq,
    drkv,
    pq_v,
    pcot_v,
    tiles,
    own_columns,
    rq_v,
    rcot_v,
    tree_k,
    tree_v,
    notes,
    picks_v,
    picks,
    pieces_in,
    picked,
    chosen,
    bias,
    self_acc,
    self_out,
    self_in,
    grads,
    shares,
    share_acc,
    totals,
    returned,
    sem_load,
    sem_note,
    sem_piece,
    sem_tile_send,
    sem_tile_recv,
    sem_pick_send,
    sem_pick_recv,
    sem_self_send,
    sem_self_recv,
    sem_share_send,
    sem_share_recv,
    sem_query,
    sem_tree,
    sem_total,
):
    scale = 1.0 / math.sqrt(HEAD_DIM)
    c = lax.axis_index("ctx")
    me = lax.axis_index("resp")
    rows = pq.shape[0]
    length = CTX * rows
    count, tokens = rq.shape[0], rq.shape[1]
    group = pq.shape[1] // (KV_HEADS * HEAD_DIM)
    width = group * HEAD_DIM
    half = KV_HEADS * HEAD_DIM
    halves, plane = cut(ring)
    size = 2 * length // plane
    blocks = rows // size
    my_half = me // plane
    my_place = lax.rem(me, plane)
    own_kind, source, own_block = held_at(blocks, my_place, c, my_half)

    def position(place):
        kind, ctx, block = held_at(blocks, place, c, my_half)
        return (kind * CTX + ctx) * blocks + block

    my_position = position(my_place)
    beside = c + 1 - 2 * lax.rem(c, 2)
    across = lax.rem(c + 2, CTX)
    x_size = 4
    y_size = plane // x_size

    def moved(step):
        x = lax.rem(lax.rem(me, x_size) + lax.rem(step, x_size), x_size)
        y = lax.rem(lax.rem(me // x_size, y_size) + lax.rem(step // x_size, y_size), y_size)
        z = lax.rem(my_half + step // plane, halves)
        return z * plane + y * x_size + x

    def remote(src, dst, send, recv, where):
        return pltpu.make_async_remote_copy(
            src_ref=src,
            dst_ref=dst,
            send_sem=send,
            recv_sem=recv,
            device_id=where,
            device_id_type=MESH,
        )

    def settle(ref, sem):
        pltpu.make_async_copy(ref, ref, sem).wait()

    own_tile = pltpu.make_async_copy(pkv, tiles.at[aligned(c * rows, rows)], sem_load.at[0])
    own_tree_k = pltpu.make_async_copy(
        rkv.at[:, :, columns(c * HEAD_DIM, HEAD_DIM)], tree_k, sem_load.at[1]
    )
    own_tree_v = pltpu.make_async_copy(
        rkv.at[:, :, columns(half + c * HEAD_DIM, HEAD_DIM)], tree_v, sem_load.at[2]
    )

    barrier = pltpu.get_barrier_semaphore()

    def greet(step, carry):
        there = (lax.rem(c + step // ring, CTX), lax.rem(me + lax.rem(step, ring), ring))
        pl.semaphore_signal(barrier, inc=1, device_id=there, device_id_type=MESH)
        return carry

    lax.fori_loop(1, CTX * ring, greet, 0)

    own_tile.start()
    own_tree_k.start()
    own_tree_v.start()

    def load_prompt_head(head, carry):
        source_columns = columns(head * HEAD_DIM, HEAD_DIM)
        place = aligned(head * rows, rows)
        pltpu.make_async_copy(pq.at[:, source_columns], pq_v.at[place], sem_load.at[3]).start()
        pltpu.make_async_copy(pcot.at[:, source_columns], pcot_v.at[place], sem_load.at[4]).start()
        return carry

    def load_response_head(head, carry):
        source_columns = columns(c * width + head * HEAD_DIM, HEAD_DIM)
        place = aligned(head * tokens, tokens)
        pltpu.make_async_copy(
            rq.at[:, :, source_columns], rq_v.at[:, place], sem_load.at[5]
        ).start()
        pltpu.make_async_copy(
            rcot.at[:, :, source_columns], rcot_v.at[:, place], sem_load.at[6]
        ).start()
        return carry

    def load_columns(index, carry):
        pltpu.make_async_copy(
            pkv.at[:, columns(index * HEAD_DIM, HEAD_DIM)], own_columns.at[index], sem_load.at[7]
        ).start()
        return carry

    lax.fori_loop(0, 2 * KV_HEADS, load_columns, 0)
    lax.fori_loop(0, KV_HEADS * group, load_prompt_head, 0)
    lax.fori_loop(0, group, load_response_head, 0)

    row = lax.broadcasted_iota(jnp.int32, (8, 128), 0)
    lane = lax.broadcasted_iota(jnp.int32, (8, 128), 1)
    note = jnp.zeros((8, 128), jnp.int32)
    inside = lane // 16 == lax.rem(me, 8)
    for r in range(count):
        route = routes_in[r]
        note = jnp.where((row == r) & inside, route * 16 + lane % 16, note)
        note = jnp.where((row == ROUTE_ROW) & (lane == r), route, note)
        note = jnp.where((row == REWARD_ROW) & (lane == r), rewards_in[r], note)
    notes[me] = note

    settle(own_columns, sem_load.at[7])
    pl.semaphore_wait(barrier, CTX * ring - 1)

    piece_count = halves * KV_HEADS * 2 * blocks

    def send_piece(step, carry):
        index = lax.rem(step + me, piece_count)
        head = lax.rem(index // (2 * blocks), KV_HEADS)
        kind = lax.rem(index, 2 * blocks) // blocks
        block = lax.rem(index, blocks)
        there_half = index // (KV_HEADS * 2 * blocks)
        place = place_of(blocks, kind, c, block, head, there_half)
        there = there_half * plane + place
        piece = own_columns.at[kind * KV_HEADS + head, aligned(block * size, size)]
        here = (head == c) & (there == me)

        @pl.when(here)
        def _():
            pltpu.make_async_copy(piece, pieces_in.at[me], sem_piece.at[2]).start()

        @pl.when(jnp.logical_not(here))
        def _():
            remote(
                piece, pieces_in.at[me], sem_piece.at[0], sem_piece.at[1], (head, there)
            ).start()

        @pl.when(step > 0)
        def _():
            note_there = (c, moved(step))
            remote(notes.at[me], notes.at[me], sem_note.at[0], sem_note.at[1], note_there).start()

        return carry

    lax.fori_loop(0, piece_count, send_piece, 0)

    def tile(index):
        return tiles.at[pl.ds(index * rows, rows)]

    def send_tile(src, index, slot, where):
        return remote(src, tile(index), sem_tile_send.at[slot], sem_tile_recv.at[index], (where, me))

    @pl.when(c == 0)
    def _():
        send_tile(pkv, 0, 0, 2).start()
        send_tile(pkv, 0, 1, 1).start()

    @pl.when(c == 1)
    def _():
        send_tile(pkv, 1, 0, 3).start()

    @pl.when(c == 2)
    def _():
        send_tile(pkv, 2, 0, 3).start()

    for index in range(1, CTX):

        @pl.when(c < index)
        def _():
            tiles[index * rows : (index + 1) * rows, :] = jnp.zeros((rows, 2 * half), jnp.bfloat16)

    stack = min(8, group)
    key = lax.broadcasted_iota(jnp.int32, (length, rows), 0)
    query = lax.broadcasted_iota(jnp.int32, (length, rows), 1) + c * rows
    allowed_here = jnp.where(key <= query, 0.0, -jnp.inf)
    for index in range(stack):
        bias[:, index * rows : (index + 1) * rows] = allowed_here
    self_acc[...] = jnp.zeros_like(self_acc)
    share_acc[...] = jnp.zeros_like(share_acc)

    settle(notes.at[pl.ds(0, ring - 1)], sem_note.at[1])
    every = notes[...]
    note_row = lax.broadcasted_iota(jnp.int32, every.shape, 1)
    routes = jnp.sum(jnp.where(note_row == ROUTE_ROW, every, 0), axis=1)
    rewards = jnp.sum(jnp.where(note_row == REWARD_ROW, every, 0), axis=1).astype(jnp.float32)
    picks_v[...] = routes
    to_scalars = pltpu.make_async_copy(picks_v, picks, sem_note.at[2])
    to_scalars.start()
    to_scalars.wait()

    @pl.when(c == source)
    def _():
        settle(pieces_in.at[me], sem_piece.at[2])
        settle(pieces_in.at[pl.ds(0, ring - 1)], sem_piece.at[1])

    @pl.when(c != source)
    def _():
        settle(pieces_in, sem_piece.at[1])

    def send_pick(step, carry):
        r = step // (plane - 1)
        there = moved(lax.rem(7 * (lax.rem(step, plane - 1) + 1), plane))
        there_place = lax.rem(there, plane)
        picked[r, there_place] = pieces_in[picks[there, r]]
        remote(
            picked.at[r, there_place],
            chosen.at[r, aligned(my_position * size, size)],
            sem_pick_send.at[r],
            sem_pick_recv.at[r],
            (c, there),
        ).start()
        return carry

    lax.fori_loop(0, count * (plane - 1), send_pick, 0)
    for r in range(count):
        chosen[r, aligned(my_position * size, size), :] = pieces_in[picks[me, r]]

    @pl.when(c == 2)
    def _():
        settle(tile(0), sem_tile_recv.at[0])
        send_tile(tile(0), 0, 1, 3).start()
        settle(tile(1), sem_tile_recv.at[1])

    @pl.when(c == 3)
    def _():
        settle(tile(1), sem_tile_recv.at[1])
        send_tile(tile(1), 1, 0, 2).start()
        settle(tile(0), sem_tile_recv.at[0])
        settle(tile(2), sem_tile_recv.at[2])

    @pl.when(c == 1)
    def _():
        settle(tile(0), sem_tile_recv.at[0])

    own_tile.wait()
    own_tree_k.wait()
    own_tree_v.wait()
    settle(pq_v, sem_load.at[3])
    settle(pcot_v, sem_load.at[4])
    settle(rq_v, sem_load.at[5])
    settle(rcot_v, sem_load.at[6])

    parts = group // stack
    together = stack * rows

    def prompt_step(step, carry):
        head = step // parts
        key_columns = columns(head * HEAD_DIM, HEAD_DIM)
        value_columns = columns(half + head * HEAD_DIM, HEAD_DIM)
        place = aligned(step * together, together)
        grad_query, ((grad_keys, grad_values),) = attention_grads(
            pq_v[place, :],
            pcot_v[place, :],
            [(tiles[:, key_columns], tiles[:, value_columns], lambda part: part + bias[...])],
            scale,
        )
        self_acc[:, key_columns] += grad_keys * scale
        self_acc[:, value_columns] += grad_values
        turned = jnp.transpose((grad_query * scale).astype(jnp.bfloat16))
        for index in range(stack):
            dpq[:, columns((step * stack + index) * HEAD_DIM, HEAD_DIM)] = turned[
                index * rows : (index + 1) * rows
            ]
        return carry

    part_width = half // PARTS

    def self_tile(index, part):
        here = slice(index * rows, (index + 1) * rows)
        keys = slice(part * part_width, (part + 1) * part_width)
        values = slice(half + part * part_width, half + (part + 1) * part_width)
        return jnp.concatenate([self_acc[here, keys], self_acc[here, values]], axis=1)

    def send_self(values, part, slot, there, there_slot):
        self_out[part, slot] = values.astype(jnp.bfloat16)
        remote(
            self_out.at[part, slot],
            self_in.at[part, there_slot],
            sem_self_send.at[part, slot],
            sem_self_recv.at[part, there_slot],
            (there, me),
        ).start()

    def prompt_part(part):
        steps = KV_HEADS * parts // PARTS
        lax.fori_loop(part * steps, (part + 1) * steps, prompt_step, 0)

        @pl.when(c == 1)
        def _():
            send_self(self_tile(0, part), part, 0, 0, 0)

        @pl.when(c == 2)
        def _():
            send_self(self_tile(1, part), part, 0, 3, 0)

        @pl.when(c == 3)
        def _():
            send_self(self_tile(0, part), part, 0, 2, 0)
            send_self(self_tile(2, part), part, 1, 2, 1)

    def cross_self(part):
        for core, index in ((2, 0), (3, 1)):

            @pl.when(c == core)
            def _():
                settle(self_in.at[part, 0], sem_self_recv.at[part, 0])
                theirs = self_in[part, 0].astype(jnp.float32)
                send_self(self_tile(index, part) + theirs, part, 2, index, 2)

    prompt_part(0)

    note_lane = lax.broadcasted_iota(jnp.int32, routes.shape, 1)
    for r in range(count):
        same = ((routes == routes_in[r]) & (note_lane < count)).astype(jnp.float32)

        def summed(values):
            return jnp.sum(jnp.sum(values, axis=1, keepdims=True), axis=0, keepdims=True)

        number = summed(same)
        reward_sum = summed(same * rewards)
        reward_square = summed(same * rewards * rewards)
        variance = reward_square * number - reward_sum * reward_sum
        spread = jnp.sqrt(jnp.maximum(variance, number * number)) / number
        own_reward = jnp.full((1, 1), rewards_in[r], jnp.int32).astype(jnp.float32)
        advantage = (own_reward - reward_sum / number) / spread
        rcot_v[r] = (advantage * rcot_v[r].astype(jnp.float32)).astype(jnp.bfloat16)

    key_place = lax.broadcasted_iota(jnp.int32, (tokens, group * tokens), 0)
    query_place = lax.broadcasted_iota(jnp.int32, (tokens, group * tokens), 1) % tokens
    square_row = lax.broadcasted_iota(jnp.int32, (tokens, tokens), 0)
    square_column = lax.broadcasted_iota(jnp.int32, (tokens, tokens), 1)

    def query_rows(r, owner):
        return drq.at[r, :, columns(owner * width, width)]

    def response_step(r, carry):
        settle(chosen.at[r, pl.ds(0, (plane - 1) * size)], sem_pick_recv.at[r])
        ends = tree_in[pl.ds(r, 1), :]
        ends = jnp.sum(
            jnp.where(square_row == square_column, ends, 0), axis=1, keepdims=True
        )
        allowed = (key_place <= query_place) & (query_place < ends)
        grad_query, (prompt_terms, tree_terms) = attention_grads(
            rq_v[r],
            rcot_v[r],
            [
                (chosen[r, :length, :], chosen[r, length:, :], None),
                (tree_k[r], tree_v[r], lambda part: jnp.where(allowed, part, -jnp.inf)),
            ],
            scale,
        )
        grads[r, :length, :] = (prompt_terms[0] * scale).astype(jnp.bfloat16)
        grads[r, length:, :] = prompt_terms[1].astype(jnp.bfloat16)
        drkv[r, :, columns(c * HEAD_DIM, HEAD_DIM)] = (tree_terms[0] * scale).astype(jnp.bfloat16)
        drkv[r, :, columns(half + c * HEAD_DIM, HEAD_DIM)] = tree_terms[1].astype(jnp.bfloat16)
        turned = jnp.transpose((grad_query * scale).astype(jnp.bfloat16))
        drq[r, :, columns(c * width, width)] = jnp.concatenate(
            [turned[g * tokens : (g + 1) * tokens] for g in range(group)], axis=1
        )

        def send_share(step, inner):
            there = moved(lax.rem(7 * step, plane))
            remote(
                grads.at[r, aligned(position(lax.rem(there, plane)) * size, size)],
                shares.at[r, my_place],
                sem_share_send.at[r],
                sem_share_recv.at[r],
                (c, there),
            ).start()
            return inner

        mine = query_rows(r, c)
        remote(mine, mine, sem_query.at[0, r], sem_query.at[1, r], (across, me)).start()
        lax.fori_loop(1, plane, send_share, 0)
        remote(mine, mine, sem_query.at[2, r], sem_query.at[3, r], (beside, me)).start()
        shares[r, my_place] = grads[r, aligned(my_position * size, size), :]
        return carry

    lax.fori_loop(0, count, response_step, 0)

    def tree_part(kind, owner):
        return drkv.at[:, :, columns(kind * half + owner * HEAD_DIM, HEAD_DIM)]

    for kind in range(2):
        mine = tree_part(kind, c)
        remote(mine, mine, sem_tree.at[0, kind], sem_tree.at[1, kind], (across, me)).start()
        remote(mine, mine, sem_tree.at[2, kind], sem_tree.at[3, kind], (beside, me)).start()

    cross_self(0)
    for part in range(1, PARTS):
        prompt_part(part)

    subs = size // 16
    groups = plane // 8

    def share_step(r, carry):
        target = lax.broadcasted_iota(jnp.int32, (ring * 16, 128), 0)
        place = lax.broadcasted_iota(jnp.int32, (8, 8, 128), 1)
        spread = []
        for index in range(groups):
            near = notes[pl.ds(my_half * plane + index * 8, 8)]
            codes = jnp.sum(jnp.where(place == r, near, 0), axis=0)
            codes = jnp.sum(codes, axis=0, keepdims=True)
            spread.append((target == codes).astype(jnp.float32).astype(jnp.bfloat16))
        spread = jnp.concatenate(spread, axis=1)
        settle(shares.at[r, pl.ds(0, plane - 1)], sem_share_recv.at[r])
        for s in range(subs):
            part = shares[r, :, s * 16 : (s + 1) * 16, :].reshape(plane * 16, HEAD_DIM)
            share_acc[s] += dot_nn(spread, part)
        theirs = query_rows(r, across)
        settle(theirs, sem_query.at[1, r])
        remote(theirs, theirs, sem_query.at[4, r], sem_query.at[5, r], (beside, me)).start()
        return carry

    def share_steps(first, last):
        lax.fori_loop(first, last, share_step, 0)

    share_steps(0, count // 2)
    for part in range(1, PARTS):
        cross_self(part)
    share_steps(count // 2, count)
    for s in range(subs):
        totals[:, s * 16 : (s + 1) * 16, :] = (
            share_acc[s].reshape(ring, 16, HEAD_DIM).astype(jnp.bfloat16)
        )

    home = returned.at[my_half, own_kind * KV_HEADS + c, aligned(own_block * size, size)]

    @pl.when(c == source)
    def _():
        pltpu.make_async_copy(totals.at[me], home, sem_total.at[2]).start()

    @pl.when(c != source)
    def _():
        remote(totals.at[me], home, sem_total.at[0], sem_total.at[1], (source, me)).start()

    def send_total(step, carry):
        there = moved(step)
        remote(
            totals.at[there], home, sem_total.at[0], sem_total.at[1], (source, there)
        ).start()
        return carry

    lax.fori_loop(1, ring, send_total, 0)

    for kind in range(2):
        theirs = tree_part(kind, across)
        settle(theirs, sem_tree.at[1, kind])
        remote(theirs, theirs, sem_tree.at[4, kind], sem_tree.at[5, kind], (beside, me)).start()

    def add_self(part, slot):
        settle(self_in.at[part, slot], sem_self_recv.at[part, slot])
        return self_in[part, slot].astype(jnp.float32)

    own_rows = pl.ds(pl.multiple_of(c * rows, rows), rows)
    for part in range(PARTS):
        keys = slice(part * part_width, (part + 1) * part_width)
        values = slice(half + part * part_width, half + (part + 1) * part_width)

        def add(more):
            self_acc[own_rows, keys] += more[:, :part_width]
            self_acc[own_rows, values] += more[:, part_width:]

        @pl.when(c == 0)
        def _():
            add(add_self(part, 0) + add_self(part, 2))

        @pl.when(c == 1)
        def _():
            add(add_self(part, 2))

        @pl.when(c == 2)
        def _():
            add(add_self(part, 1))

        @pl.when(c >= 1)
        def _():
            settle(self_out.at[part, 0], sem_self_send.at[part, 0])

        @pl.when(c == 3)
        def _():
            settle(self_out.at[part, 1], sem_self_send.at[part, 1])

        @pl.when(c >= 2)
        def _():
            settle(self_out.at[part, 2], sem_self_send.at[part, 2])

    settle(notes.at[pl.ds(0, ring - 1)], sem_note.at[0])

    @pl.when(c == source)
    def _():
        settle(pieces_in.at[pl.ds(0, piece_count - 1)], sem_piece.at[0])

    @pl.when(c != source)
    def _():
        settle(pieces_in.at[pl.ds(0, piece_count)], sem_piece.at[0])

    @pl.when(c == 0)
    def _():
        send_tile(pkv, 0, 0, 2).wait_send()
        send_tile(pkv, 0, 1, 1).wait_send()

    @pl.when(c == 1)
    def _():
        send_tile(pkv, 1, 0, 3).wait_send()

    @pl.when(c == 2)
    def _():
        send_tile(pkv, 2, 0, 3).wait_send()
        send_tile(tile(0), 0, 1, 3).wait_send()

    @pl.when(c == 3)
    def _():
        send_tile(tile(1), 1, 0, 2).wait_send()

    for r in range(count):
        settle(picked.at[r, pl.ds(0, plane - 1)], sem_pick_send.at[r])
        settle(shares.at[r, pl.ds(0, plane - 1)], sem_share_send.at[r])
        for slot in (0, 2, 3, 4, 5):
            settle(query_rows(r, c), sem_query.at[slot, r])
    for kind in range(2):
        for slot in (0, 2, 3, 4, 5):
            settle(tree_part(kind, c), sem_tree.at[slot, kind])

    @pl.when(c == source)
    def _():
        settle(totals.at[me], sem_total.at[2])
        settle(totals.at[pl.ds(0, ring - 1)], sem_total.at[0])

    @pl.when(c != source)
    def _():
        settle(totals, sem_total.at[0])

    others = halves * KV_HEADS * 2 * blocks

    @pl.when(c == source)
    def _():
        settle(totals.at[pl.ds(0, others - 1)], sem_total.at[1])

    @pl.when(c != source)
    def _():
        settle(totals.at[pl.ds(0, others)], sem_total.at[1])

    for index in range(2 * KV_HEADS):
        here = slice(index * HEAD_DIM, (index + 1) * HEAD_DIM)
        total = self_acc[own_rows, here]
        for z in range(halves):
            total = total + returned[z, index].astype(jnp.float32)
        dpkv[:, here] = total.astype(jnp.bfloat16)


def store(count, *refs):
    sources, targets, sems = refs[:count], refs[count : 2 * count], refs[2 * count]
    copies = [
        pltpu.make_async_copy(source, target, sems.at[index])
        for index, (source, target) in enumerate(zip(sources, targets))
    ]
    for copy in copies:
        copy.start()
    for copy in copies:
        copy.wait()


def body(
    prompt_q, prompt_kv, prompt_cot, resp_q, resp_kv, resp_cot, resp_prompt, tree_end, rewards
):
    ring = lax.axis_size("resp")
    rows, wide = prompt_q.shape[1:]
    kv_wide = prompt_kv.shape[2]
    count, tokens = resp_q.shape[:2]
    length = CTX * rows
    group = wide // (KV_HEADS * HEAD_DIM)
    width = group * HEAD_DIM
    halves, plane = cut(ring)
    size = 2 * length // plane
    bf16, f32, i32 = jnp.bfloat16, jnp.float32, jnp.int32
    any_space = pl.BlockSpec(memory_space=pl.ANY)
    scalars = pl.BlockSpec(memory_space=pltpu.SMEM)
    vector = pl.BlockSpec(memory_space=pltpu.VMEM)
    dma = pltpu.SemaphoreType.DMA
    dpq, dpkv, drq, drkv = pl.pallas_call(
        functools.partial(kernel, ring),
        out_shape=(
            pltpu.VMEM((rows, wide), bf16),
            pltpu.VMEM((rows, kv_wide), bf16),
            pltpu.VMEM(resp_q.shape, bf16),
            pltpu.VMEM(resp_kv.shape, bf16),
        ),
        in_specs=[scalars, scalars, vector] + [any_space] * 6,
        out_specs=(vector,) * 4,
        scratch_shapes=[
            pltpu.VMEM((wide // HEAD_DIM * rows, HEAD_DIM), bf16),
            pltpu.VMEM((wide // HEAD_DIM * rows, HEAD_DIM), bf16),
            pltpu.VMEM((length, kv_wide), bf16),
            pltpu.VMEM((kv_wide // HEAD_DIM, rows, HEAD_DIM), bf16),
            pltpu.VMEM((count, group * tokens, HEAD_DIM), bf16),
            pltpu.VMEM((count, group * tokens, HEAD_DIM), bf16),
            pltpu.VMEM((count, tokens, HEAD_DIM), bf16),
            pltpu.VMEM((count, tokens, HEAD_DIM), bf16),
            pltpu.VMEM((ring, 8, 128), i32),
            pltpu.VMEM((ring, 128), i32),
            pltpu.SMEM((ring, 128), i32),
            pltpu.VMEM((ring, size, HEAD_DIM), bf16),
            pltpu.VMEM((count, plane, size, HEAD_DIM), bf16),
            pltpu.VMEM((count, 2 * length, HEAD_DIM), bf16),
            pltpu.VMEM((length, min(8, group) * rows), f32),
            pltpu.VMEM((length, kv_wide), f32),
            pltpu.VMEM((PARTS, 3, rows, kv_wide // PARTS), bf16),
            pltpu.VMEM((PARTS, 3, rows, kv_wide // PARTS), bf16),
            pltpu.VMEM((count, 2 * length, HEAD_DIM), bf16),
            pltpu.VMEM((count, plane, size, HEAD_DIM), bf16),
            pltpu.VMEM((size // 16, ring * 16, HEAD_DIM), f32),
            pltpu.VMEM((ring, size, HEAD_DIM), bf16),
            pltpu.VMEM((halves, kv_wide // HEAD_DIM, rows, HEAD_DIM), bf16),
            dma((8,)),
            dma((3,)),
            dma((3,)),
            dma((2,)),
            dma((CTX,)),
            dma((count,)),
            dma((count,)),
            dma((PARTS, 3)),
            dma((PARTS, 3)),
            dma((count,)),
            dma((count,)),
            dma((6, count)),
            dma((6, 2)),
            dma((3,)),
        ],
        compiler_params=pltpu.CompilerParams(
            collective_id=0, has_side_effects=True, vmem_limit_bytes=52 * 1024 * 1024
        ),
        name="attention_gradients",
    )(
        resp_prompt[:, 0],
        rewards,
        tree_end,
        prompt_q[0],
        prompt_kv[0],
        prompt_cot[0],
        resp_q,
        resp_kv,
        resp_cot,
    )
    results = (dpq, dpkv, drq, drkv)
    dpq, dpkv, drq, drkv = pl.pallas_call(
        functools.partial(store, len(results)),
        out_shape=[jax.ShapeDtypeStruct(result.shape, result.dtype) for result in results],
        in_specs=[vector] * len(results),
        out_specs=[any_space] * len(results),
        scratch_shapes=[dma((len(results),))],
        compiler_params=pltpu.CompilerParams(vmem_limit_bytes=16 * 1024 * 1024),
        name="store_outputs",
    )(*results)
    return (dpq[None], dpkv[None], drq, drkv)


def solution(mesh):
    in_specs = (
        P("resp", "ctx", None),
        P("resp", "ctx", None),
        P("resp", "ctx", None),
        P("resp", None, None),
        P("resp", None, None),
        P("resp", None, None),
        P("resp", None),
        P("resp", None),
        P("resp"),
    )
    out_specs = (
        P("resp", "ctx", None),
        P("resp", "ctx", None),
        P("resp", None, None),
        P("resp", None, None),
    )
    return jax.shard_map(body, mesh=mesh, in_specs=in_specs, out_specs=out_specs, check_vma=False)
```
